256 devices in a mesh: dom: 32 (over z, x), tp: 8 (over y, core).
Axes of the slice: x: 4, y: 4, z: 8, core: 2. Of those that a mesh axis runs over, the one named last changes fastest.
Arguments:
- queries: bfloat16 [1024, 8192], P('dom', 'tp'), may hold values from -12 to 12
- new_keys: bfloat16 [1024, 1024], P('dom', 'tp'), may hold values from -12 to 12
- new_values: bfloat16 [1024, 1024], P('dom', 'tp'), may hold values from -6 to 6
- cache_keys: bfloat16 [1024, 256, 1024], P('dom', None, 'tp'), may hold values from -12 to 12
- cache_values: bfloat16 [1024, 256, 1024], P('dom', None, 'tp'), may hold values from -6 to 6
- ancestors: int32 [1024], replicated, may hold values from 0 to 1023, as said below
- out_weight: bfloat16 [8192, 8192], P('tp', 'dom'), may hold values from -0.0625 to 0.0625
Outputs:
- mixed: bfloat16 [1024, 8192], P('tp', 'dom')
The draws below stay inside these ranges and needn't reach their ends.
Inputs may be any that keep to these rules, and one draw needn't show every extreme that they name: Each group of 32 consecutive particles has at most 2 distinct ancestors among the particles of any one group, and every group has exactly 2 in some group; a few particles are ancestors of many.
All inputs are finite; a program needn't handle non-finite values.
Results may differ from the reference program's by a relative error of at most 0.0052.
Values may be sent and summed in bfloat16 or wider, within the bound.
No kernel may reach another device: no remote copies, remote signals or barrier semaphores. Data moves between devices by JAX's collectives and lax.ppermute only.
A program may use at most 64 MiB of HBM per device.

```python
import math
import jax
import jax.numpy as jnp
from jax import lax

D = 8192
H = 64
KVH = 8
HD = 128
PART_DEV = 32
CTX = 256
CAP = 2
PARTICLES = 1024


def lineage(key):
    group_total = PARTICLES // PART_DEV
    streams = jax.random.split(jax.random.fold_in(key, 5), 10)
    members = jnp.arange(PART_DEV, dtype=jnp.int32)
    favored = jax.random.randint(streams[0], (group_total,), 0, PART_DEV)
    spread = jax.random.randint(streams[1], (group_total, group_total, PART_DEV - 1), 0, 1 << 20) * (PART_DEV - 1)
    spread = spread + jnp.arange(PART_DEV - 1, dtype=jnp.int32)
    others = jnp.argsort(spread, axis=-1)[..., :CAP - 1].astype(jnp.int32)
    others = others + (others >= favored[None, :, None]).astype(jnp.int32)
    leading_dims = jnp.broadcast_to(favored[None, :, None], (group_total, group_total, 1))
    candidates = jnp.concatenate([leading_dims, others], axis=-1)
    heavy = jax.random.randint(streams[2], (4,), 0, group_total)
    uniform_src = jax.random.randint(streams[3], (group_total, PART_DEV), 0, group_total)
    heavy_src = heavy[jax.random.randint(streams[4], (group_total, PART_DEV), 0, 4)]
    source = jnp.where(jax.random.randint(streams[5], (group_total, PART_DEV), 0, 4) == 0, heavy_src, uniform_src)
    picked_slot = jnp.where(jax.random.randint(streams[6], (group_total, PART_DEV), 0, 2) == 0, jax.random.randint(streams[7], (group_total, PART_DEV), 0, CAP), 0)
    shift_by = jax.random.randint(streams[8], (group_total,), 0, group_total)
    forced = members < CAP
    group_ids = jnp.arange(group_total, dtype=jnp.int32)
    source = jnp.where(forced[None, :], (group_ids[:, None] + shift_by[:, None]) % group_total, source)
    picked_slot = jnp.where(forced[None, :], jnp.minimum(members, CAP - 1)[None, :], picked_slot)
    shuffle_keys = jax.random.randint(streams[9], (group_total, PART_DEV), 0, 1 << 20) * PART_DEV + members[None, :]
    shuffle = jnp.argsort(shuffle_keys, axis=1)
    source = jnp.take_along_axis(source, shuffle, axis=1)
    picked_slot = jnp.take_along_axis(picked_slot, shuffle, axis=1)
    slot_in_group = candidates[group_ids[:, None], source, picked_slot]
    return (source * PART_DEV + slot_in_group).reshape(PARTICLES).astype(jnp.int32)


def draw_ancestors(key, part):
    parents = lineage(key)
    return parents


def draw_queries(key, part):
    key = jax.random.fold_in(key, 11)
    result = jnp.clip(jax.random.normal(key, (PARTICLES, H * HD)), -6.0, 6.0)
    return result.astype(jnp.bfloat16)


def draw_new_keys(key, part):
    key = jax.random.fold_in(key, 13)
    result = jnp.clip(3.0 * jax.random.normal(key, (PARTICLES, KVH * HD)), -9.0, 9.0)
    return result.astype(jnp.bfloat16)


def draw_cache_keys(key, part):
    key = jax.random.fold_in(key, 17)
    result = jnp.clip(jax.random.normal(key, (PARTICLES, CTX, KVH * HD)), -6.0, 6.0)
    return result.astype(jnp.bfloat16)


def steps_of(rng, dims, cuts, smallest, high):
    def one(position, shards_of):
        draws = jax.random.uniform(jax.random.fold_in(jax.random.fold_in(rng, 6), position), (shards_of,), jnp.float32, smallest / len(cuts), high / len(cuts))
        return jnp.repeat(jnp.exp(draws), dims[position] // shards_of).reshape((-1,) + (1,) * (len(dims) - position - 1))

    gain = one(*cuts[0])
    for cut in cuts[1:]:
        gain = gain * one(*cut)
    return gain


def scatter_about(rng, shape, deviation, limit, shards=(), kind=jnp.bfloat16):
    values = deviation * jax.random.normal(rng, shape, jnp.float32)
    if shards:
        values = values * steps_of(rng, shape, shards, -0.22, 0.18)
    return jnp.clip(values, -limit, limit).astype(kind)


def setup_inputs(seed: int = 0) -> dict:
    arg_keys = jax.random.split(jax.random.key(seed), 8)
    queries = draw_queries(jax.random.fold_in(arg_keys[7], 71), 0)
    new_keys = draw_new_keys(jax.random.fold_in(arg_keys[7], 71), 0)
    new_values = scatter_about(arg_keys[2], (PARTICLES, KVH * HD), 1.0, 6.0, ((0, 32), (1, 8)))
    cache_keys = draw_cache_keys(jax.random.fold_in(arg_keys[7], 71), 0)
    cache_values = scatter_about(arg_keys[4], (PARTICLES, CTX, KVH * HD), 1.0, 6.0, ((0, 32), (2, 8)))
    ancestors = draw_ancestors(jax.random.fold_in(arg_keys[7], 71), 0)
    out_weight = scatter_about(arg_keys[6], (H * HD, D), (H * HD) ** -0.5, 0.0625, ((0, 8), (1, 32)))
    return dict(queries=queries, new_keys=new_keys, new_values=new_values, cache_keys=cache_keys, cache_values=cache_values, ancestors=ancestors, out_weight=out_weight)


def attend(query_rows, new_key_rows, new_value_rows, past_keys, past_values):
    batch = query_rows.shape[0]
    kv_heads = new_key_rows.shape[1] // HD
    per_group = query_rows.shape[1] // HD // kv_heads
    length = past_keys.shape[1]
    scaling_factor = 1.0 / math.sqrt(HD)
    queries_float32 = query_rows.astype(jnp.float32).reshape(batch, kv_heads, per_group, HD)
    keys_float32 = past_keys.astype(jnp.float32).reshape(batch, length, kv_heads, HD)
    latest_key = new_key_rows.astype(jnp.float32).reshape(batch, kv_heads, HD)
    past_scores = jnp.einsum('bkgd,btkd->bkgt', queries_float32, keys_float32) * scaling_factor
    diagonal_scores = jnp.einsum('mpix,mpx->mpi', queries_float32, latest_key) * scaling_factor
    row_max = jnp.maximum(lax.optimization_barrier(jnp.max(past_scores, axis=-1)), diagonal_scores)
    past_weights = jnp.exp(past_scores - row_max[..., None])
    self_weights = jnp.exp(diagonal_scores - row_max)
    totals = lax.optimization_barrier(jnp.sum(past_weights, axis=-1)) + self_weights
    past_rounded = lax.optimization_barrier(past_weights.astype(jnp.bfloat16)).astype(jnp.float32)
    self_rounded = lax.optimization_barrier(self_weights.astype(jnp.bfloat16)).astype(jnp.float32)
    values32 = past_values.astype(jnp.float32).reshape(batch, length, kv_heads, HD)
    fresh_value = new_value_rows.astype(jnp.float32).reshape(batch, kv_heads, 1, HD)
    mixture = jnp.einsum('bkgt,btkd->bkgd', past_rounded, values32) + self_rounded[..., None] * fresh_value
    return (mixture / totals[..., None]).astype(jnp.bfloat16).reshape(batch, kv_heads * per_group * HD)

def reference(queries, new_keys, new_values, cache_keys, cache_values, ancestors, out_weight):

    def one_group(group_index):
        offset = group_index * PART_DEV
        parents = lax.dynamic_slice_in_dim(ancestors, offset, PART_DEV).astype(jnp.int32)
        past_keys = jnp.take(cache_keys, parents, axis=0)
        past_values = jnp.take(cache_values, parents, axis=0)
        return attend(lax.dynamic_slice_in_dim(queries, offset, PART_DEV), lax.dynamic_slice_in_dim(new_keys, offset, PART_DEV), lax.dynamic_slice_in_dim(new_values, offset, PART_DEV), past_keys, past_values)
    heads_out = lax.map(one_group, jnp.arange(PARTICLES // PART_DEV, dtype=jnp.int32))
    heads_out = heads_out.reshape(PARTICLES, H * HD)
    return jnp.dot(heads_out, out_weight, preferred_element_type=jnp.float32).astype(jnp.bfloat16)
```

```python
import functools
import math

import jax
import jax.numpy as jnp
from jax import lax
from jax.experimental import pallas as pl
from jax.experimental.pallas import tpu as pltpu
from jax.sharding import Mesh, PartitionSpec as P

HD = 128
ROWS = 16
BLOCKS = 8
LANES = 128
VMEM = pltpu.VMEM
F32 = jnp.float32
BF16 = jnp.bfloat16


def iota(shape, dim):
    return lax.broadcasted_iota(jnp.int32, shape, dim)


def dot(a, b):
    return jnp.dot(a, b, preferred_element_type=F32)


def dot_tn(a, b):
    return lax.dot_general(a, b, (((0,), (0,)), ((), ())), preferred_element_type=F32)


def dot_nt(a, b):
    return lax.dot_general(a, b, (((1,), (1,)), ((), ())), preferred_element_type=F32)


def pack_kernel(row_ref, q_ref, k_ref, v_ref, out_ref):
    slots = out_ref.shape[0]
    members = q_ref.shape[0]
    width = q_ref.shape[1]
    pick = (iota((slots, members), 0) == row_ref[0:1, :members]).astype(BF16)
    out_ref[:, :width] = dot(pick, q_ref[...]).astype(BF16)
    out_ref[:, width : width + HD] = dot(pick, k_ref[...]).astype(BF16)
    out_ref[:, width + HD :] = dot(pick, v_ref[...]).astype(BF16)


def attend_kernel(
    cap, cap_out, tables_ref, recv_ref, keys_ref, values_ref, out_ref,
    keys, values, order, order_smem, total, sems, order_sem,
):
    load_keys = pltpu.make_async_copy(keys_ref, keys, sems.at[0])
    load_values = pltpu.make_async_copy(values_ref, values, sems.at[1])
    load_keys.start()
    load_values.start()
    rows = recv_ref.shape[0]
    groups = tables_ref.shape[0]
    heads = (recv_ref.shape[1] - 2 * HD) // HD
    scale = 1.0 / math.sqrt(HD)

    repeat = (iota((rows, groups), 0) // cap == iota((rows, groups), 1)).astype(BF16)
    spread = dot(repeat, tables_ref[...])
    hit = spread[:, :LANES] == (iota((rows, LANES), 0) % cap).astype(F32)
    found = jnp.sum(jnp.where(hit, 1.0, 0.0), axis=1, keepdims=True) > 0.5
    local = jnp.sum(jnp.where(hit, spread[:, LANES : 2 * LANES], 0.0), axis=1, keepdims=True)
    place = jnp.sum(
        jnp.where(hit, spread[:, 2 * LANES : 3 * LANES] * cap_out + spread[:, 3 * LANES :], 0.0),
        axis=1,
        keepdims=True,
    )
    local = jnp.where(found, local, -1.0)
    place = jnp.where(found, place, -1.0)

    member = (local == iota((rows, LANES), 1).astype(F32)).astype(F32)
    member16 = member.astype(BF16)
    before = (iota((rows, rows), 1) < iota((rows, rows), 0)).astype(BF16)
    rank = dot(before, member16)
    count = jnp.sum(member, axis=0, keepdims=True)
    blocks = jnp.floor((count + (ROWS - 1)) * (1.0 / ROWS))
    upto = (iota((LANES, LANES), 0) < iota((LANES, LANES), 1)).astype(BF16)
    first = dot(jnp.broadcast_to(blocks, (8, LANES)).astype(BF16), upto)[0:1]
    position = jnp.sum(member * (rank + first * ROWS), axis=1, keepdims=True)
    position = jnp.where(found, position, -1.0)
    steps = (jnp.sum(blocks).astype(jnp.int32) + BLOCKS - 1) // BLOCKS
    ended = (first + blocks) <= iota((LANES, LANES), 0).astype(F32)
    owner = jnp.sum(jnp.where(ended & (iota((LANES, LANES), 1) < groups), 1.0, 0.0), axis=1, keepdims=True)
    owner = jnp.minimum(owner, groups - 1.0)
    order[...] = jnp.transpose(jnp.broadcast_to(owner, (LANES, LANES)))[0:8].astype(jnp.int32)
    move = pltpu.make_async_copy(order, order_smem, order_sem)
    move.start()
    target = (place == iota((rows, out_ref.shape[0]), 1).astype(F32)).astype(BF16)
    total[...] = jnp.zeros_like(total)
    move.wait()
    load_keys.wait()
    load_values.wait()

    def step(k, carry):
        base = (k * (BLOCKS * ROWS)).astype(F32)
        taken = (position - base == iota((rows, BLOCKS * ROWS), 1).astype(F32)).astype(BF16)
        gathered = dot_tn(taken, recv_ref[...]).astype(BF16)
        results = []
        for b in range(BLOCKS):
            ancestor = order_smem[0, k * BLOCKS + b]
            part = gathered[b * ROWS : (b + 1) * ROWS]
            query = jnp.concatenate([part[:, h * HD : (h + 1) * HD] for h in range(heads)], axis=0)
            new_key = jnp.concatenate([part[:, heads * HD : (heads + 1) * HD]] * heads, axis=0)
            new_value = jnp.concatenate([part[:, (heads + 1) * HD :]] * heads, axis=0)
            past = dot_nt(query, keys[ancestor]) * scale
            own = jnp.sum(query.astype(F32) * new_key.astype(F32), axis=1, keepdims=True) * scale
            top = jnp.maximum(jnp.max(past, axis=1, keepdims=True), own)
            weight = jnp.exp(past - top)
            own = jnp.exp(own - top)
            norm = jnp.sum(weight, axis=1, keepdims=True) + own
            mix = dot(weight.astype(BF16), values[ancestor])
            mix = mix + own.astype(BF16).astype(F32) * new_value.astype(F32)
            mix = (mix / norm).astype(BF16)
            results.append(
                jnp.concatenate([mix[h * ROWS : (h + 1) * ROWS] for h in range(heads)], axis=1)
            )
        result = jnp.concatenate(results, axis=0)
        send = dot_tn(target, taken).astype(BF16)
        total[...] += dot(send, result)
        return carry

    lax.fori_loop(0, steps, step, 0)
    out_ref[...] = total[...].astype(BF16)


def on_device(queries, new_keys, new_values, cache_keys, cache_values, ancestors, out_weight):
    groups = lax.axis_size("z") * lax.axis_size("x")
    lines = lax.axis_size("z")
    cross = lax.axis_size("x")
    z = lax.axis_index("z")
    x = lax.axis_index("x")
    position = z * cross + x
    out_line = lax.axis_index("y") * lax.axis_size("core") + lax.axis_index("core")
    members, length, width = cache_keys.shape
    span = cross * members
    everything = queries.shape[1] + 2 * HD

    weights = lax.all_gather(out_weight, "x", axis=0)

    source = (ancestors // members).reshape(groups, members)
    local = (ancestors % members).reshape(groups, members)
    earlier = iota((members, members), 1) < iota((members, members), 0)
    slot = jnp.sum(
        ((source[:, :, None] == source[:, None, :]) & earlier[None]).astype(jnp.int32), axis=2
    )
    line_source = source.reshape(lines, span)
    line_key = line_source * span + jnp.arange(span, dtype=jnp.int32)
    sorted_at = jnp.sum((line_key[:, None, :] < line_key[:, :, None]).astype(jnp.int32), axis=2)
    run_start = jnp.sum((line_source[:, None, :] < line_source[:, :, None]).astype(jnp.int32), axis=2)
    slot_out = (sorted_at - run_start) // cross
    need = jnp.max(slot) + 1
    need_out = jnp.max(slot_out) + 1
    target = jnp.arange(lines, dtype=jnp.int32)[:, None] * cross + sorted_at % cross

    mine = source == position
    pad = lambda a: jnp.pad(a.astype(BF16), ((0, 0), (0, LANES - members)), constant_values=-1)
    tables = jnp.concatenate(
        [
            pad(jnp.where(mine, slot, -1)),
            pad(local),
            pad(target.reshape(groups, members)),
            pad(slot_out.reshape(groups, members)),
        ],
        axis=1,
    )
    own_source = lax.dynamic_index_in_dim(source, position, 0, False)
    own_slot = lax.dynamic_index_in_dim(slot, position, 0, False)
    here_source = lax.dynamic_index_in_dim(line_source, z, 0, False)
    here_slot = lax.dynamic_index_in_dim(slot_out, z, 0, False)
    here_at = lax.dynamic_index_in_dim(sorted_at, z, 0, False)
    wanted = here_at[None, :] == (jnp.arange(members, dtype=jnp.int32) * cross + x)[:, None]

    def exchange(cap, cap_out):
        row = jnp.broadcast_to((own_source * cap + own_slot)[None, :], (8, members))
        sent = pl.pallas_call(
            pack_kernel,
            out_shape=jax.ShapeDtypeStruct((groups * cap, everything), BF16),
            in_specs=[pl.BlockSpec(memory_space=VMEM)] * 4,
            out_specs=pl.BlockSpec(memory_space=VMEM),
            name="pack",
        )(row, queries, new_keys, new_values)
        received = lax.all_to_all(
            sent.reshape(groups, cap, everything), ("z", "x"), 0, 0, tiled=True
        ).reshape(groups * cap, everything)
        mixed = pl.pallas_call(
            functools.partial(attend_kernel, cap, cap_out),
            out_shape=jax.ShapeDtypeStruct((groups * cap_out, queries.shape[1]), BF16),
            in_specs=[pl.BlockSpec(memory_space=VMEM)] * 2 + [pl.BlockSpec(memory_space=pl.ANY)] * 2,
            out_specs=pl.BlockSpec(memory_space=VMEM),
            scratch_shapes=[
                pltpu.VMEM(cache_keys.shape, BF16),
                pltpu.VMEM(cache_values.shape, BF16),
                pltpu.VMEM((8, LANES), jnp.int32),
                pltpu.SMEM((8, LANES), jnp.int32),
                pltpu.VMEM((groups * cap_out, queries.shape[1]), F32),
                pltpu.SemaphoreType.DMA((2,)),
                pltpu.SemaphoreType.DMA,
            ],
            compiler_params=pltpu.CompilerParams(vmem_limit_bytes=40 << 20),
            name="attend",
        )(tables, received, cache_keys, cache_values)
        returned = lax.all_to_all(
            mixed.reshape(groups, cap_out, queries.shape[1]), ("z", "x"), 0, 0, tiled=True
        ).reshape(groups * cap_out, queries.shape[1])
        origin = jnp.sum(jnp.where(wanted, here_source * cap_out + here_slot, 0), axis=1)
        origin = jnp.tile(origin, lines)
        choose = origin[:, None] == jnp.arange(groups * cap_out, dtype=jnp.int32)[None, :]
        return dot(choose.astype(BF16), returned).astype(BF16)

    level = jnp.where((need <= 8) & (need_out <= 8), 0, jnp.where((need <= 16) & (need_out <= 8), 1, 2))
    heads_out = lax.switch(
        level,
        [
            functools.partial(exchange, 8, 8),
            functools.partial(exchange, 16, 8),
            functools.partial(exchange, members, members),
        ],
    )

    column = lax.all_to_all(
        heads_out.reshape(lines, members, queries.shape[1]), "z", 0, 0, tiled=True
    ).reshape(lines * members, queries.shape[1])
    partial_rows = jnp.einsum("rk,xkn->xrn", column, weights, preferred_element_type=F32).astype(BF16)
    columns = out_weight.shape[1]
    shares = lax.all_to_all(
        partial_rows.reshape(cross * lines, members, columns), ("x", "y", "core"), 0, 0, tiled=True
    )
    summed = jnp.sum(shares.reshape(cross, lines, members, columns).astype(F32), axis=1)
    summed = summed.reshape(span, columns).astype(BF16)
    out_at = lax.dynamic_index_in_dim(sorted_at, out_line, 0, False)
    restore = ((out_at % cross) * members + out_at // cross)[:, None] == jnp.arange(span, dtype=jnp.int32)
    return dot(restore.astype(BF16), summed).astype(BF16)


def solution(mesh):
    inner = Mesh(mesh.devices.reshape(8, 4, 4, 2), ("z", "x", "y", "core"))
    dom = ("z", "x")
    tp = ("y", "core")
    return jax.shard_map(
        on_device,
        mesh=inner,
        in_specs=(P(dom, tp), P(dom, tp), P(dom, tp), P(dom, None, tp), P(dom, None, tp), P(), P(tp, dom)),
        out_specs=P(tp, dom),
        check_vma=False,
    )
```

```python
import functools
import math

import jax
import jax.numpy as jnp
from jax import lax
from jax.experimental import pallas as pl
from jax.experimental.pallas import tpu as pltpu
from jax.sharding import Mesh, PartitionSpec as P

HD = 128
ROWS = 16
BLOCKS = 8
LANES = 128
FIRST = 8
VMEM = pltpu.VMEM
F32 = jnp.float32
BF16 = jnp.bfloat16
DOM = ("z", "x")
TP = ("y", "core")


def iota(shape, dim):
    return lax.broadcasted_iota(jnp.int32, shape, dim)


def dot(a, b):
    return jnp.dot(a, b, preferred_element_type=F32)


def dot_tn(a, b):
    return lax.dot_general(a, b, (((0,), (0,)), ((), ())), preferred_element_type=F32)


def dot_nt(a, b):
    return lax.dot_general(a, b, (((1,), (1,)), ((), ())), preferred_element_type=F32)


def call(body, name, *, out, n_vmem, n_any=0, scratch=(), limit=24, out_specs=None):
    return pl.pallas_call(
        body,
        out_shape=out,
        in_specs=[pl.BlockSpec(memory_space=VMEM)] * n_vmem + [pl.BlockSpec(memory_space=pl.ANY)] * n_any,
        out_specs=out_specs or pl.BlockSpec(memory_space=VMEM),
        scratch_shapes=scratch,
        compiler_params=pltpu.CompilerParams(vmem_limit_bytes=limit << 20),
        name=name,
    )


def fill(pick, q_ref, k_ref, v_ref, out_ref):
    width = q_ref.shape[1]
    out_ref[:, :width] = dot(pick, q_ref[...]).astype(BF16)
    out_ref[:, width : width + HD] = dot(pick, k_ref[...]).astype(BF16)
    out_ref[:, width + HD :] = dot(pick, v_ref[...]).astype(BF16)


def picks(own_ref, cap, slots, members):
    row = own_ref[0:1, :members] * cap + own_ref[8:9, :members]
    return (iota((slots, members), 0) == row).astype(BF16)


def prepare_kernel(cross, anc_ref, q_ref, k_ref, v_ref, sent_ref, own_ref, tables_ref, need_ref):
    lines = anc_ref.shape[0]
    members = q_ref.shape[0]
    groups = lines * cross
    z, x = lax.axis_index("z"), lax.axis_index("x")
    anc = jnp.concatenate(
        [anc_ref[...]] + [pltpu.roll(anc_ref[...], LANES - members * j, 1) for j in range(1, cross)], axis=0
    )
    inside = iota((groups, LANES), 1) < members
    source = jnp.where(inside, anc // members, -1)
    local = anc % members
    lane = iota((groups, LANES), 1)
    slot = jnp.zeros((groups, LANES), jnp.int32)
    for k in range(1, members):
        slot += ((source == pltpu.roll(source, k, 1)) & (lane >= k)).astype(jnp.int32)
    slot = jnp.where(inside, slot, 0)
    need_ref[0] = jnp.max(slot) + 1
    mine = source == z * cross + x
    tables_ref[:, :LANES] = jnp.where(mine, slot, -1).astype(F32).astype(BF16)
    tables_ref[:, LANES:] = jnp.where(mine, local, 0).astype(F32).astype(BF16)
    here = iota((groups, LANES), 0) == x * lines + z
    own_ref[0:8] = jnp.broadcast_to(jnp.sum(jnp.where(here, source, 0), axis=0, keepdims=True), (8, LANES))
    own_ref[8:16] = jnp.broadcast_to(jnp.sum(jnp.where(here, slot, 0), axis=0, keepdims=True), (8, LANES))
    fill(picks(own_ref, FIRST, groups * FIRST, members), q_ref, k_ref, v_ref, sent_ref)


def pack_kernel(cap, own_ref, q_ref, k_ref, v_ref, sent_ref):
    fill(picks(own_ref, cap, sent_ref.shape[0], q_ref.shape[0]), q_ref, k_ref, v_ref, sent_ref)


def unpack_kernel(cap, own_ref, returned_ref, out_ref):
    members = out_ref.shape[-2]
    pick = picks(own_ref, cap, returned_ref.shape[0], members)
    rows = dot_tn(pick, returned_ref[...]).astype(BF16)
    for i in range(out_ref.shape[0]):
        out_ref[i] = rows


def attend_kernel(
    cap, cross, tables_ref, recv_ref, keys_ref, values_ref, out_ref,
    keys, values, order, order_smem, total, sems, order_sem,
):
    load_keys = pltpu.make_async_copy(keys_ref, keys, sems.at[0])
    load_values = pltpu.make_async_copy(values_ref, values, sems.at[1])
    load_keys.start()
    load_values.start()
    rows = recv_ref.shape[0]
    groups = tables_ref.shape[0]
    lines = groups // cross
    heads = (recv_ref.shape[1] - 2 * HD) // HD
    scale = 1.0 / math.sqrt(HD)

    group = iota((rows, groups), 0) // cap
    repeat = ((group % cross) * lines + group // cross == iota((rows, groups), 1)).astype(BF16)
    spread = dot(repeat, tables_ref[...])
    hit = spread[:, :LANES] == (iota((rows, LANES), 0) % cap).astype(F32)
    local = jnp.sum(jnp.where(hit, spread[:, LANES:] + 1.0, 0.0), axis=1, keepdims=True) - 1.0

    member = (local == iota((rows, LANES), 1).astype(F32)).astype(F32)
    before = (iota((rows, rows), 1) < iota((rows, rows), 0)).astype(BF16)
    rank = dot(before, member.astype(BF16))
    count = jnp.sum(member, axis=0, keepdims=True)
    blocks = jnp.floor((count + (ROWS - 1)) * (1.0 / ROWS))
    upto = (iota((LANES, LANES), 0) < iota((LANES, LANES), 1)).astype(BF16)
    first = dot(jnp.broadcast_to(blocks, (8, LANES)).astype(BF16), upto)[0:1]
    position = jnp.sum(member * (rank + first * ROWS), axis=1, keepdims=True)
    position = jnp.where(local >= 0.0, position, -1.0)
    steps = (jnp.sum(blocks).astype(jnp.int32) + BLOCKS - 1) // BLOCKS
    ended = (first + blocks) <= iota((LANES, LANES), 0).astype(F32)
    owner = jnp.sum(jnp.where(ended & (iota((LANES, LANES), 1) < groups), 1.0, 0.0), axis=1, keepdims=True)
    owner = jnp.minimum(owner, groups - 1.0)
    order[...] = jnp.transpose(jnp.broadcast_to(owner, (LANES, LANES)))[0:8].astype(jnp.int32)
    move = pltpu.make_async_copy(order, order_smem, order_sem)
    move.start()
    total[...] = jnp.zeros_like(total)
    move.wait()
    load_keys.wait()
    load_values.wait()

    def step(k, carry):
        base = (k * (BLOCKS * ROWS)).astype(F32)
        taken = (position - base == iota((rows, BLOCKS * ROWS), 1).astype(F32)).astype(BF16)
        gathered = dot_tn(taken, recv_ref[...]).astype(BF16)
        results = []
        for b in range(BLOCKS):
            ancestor = order_smem[0, k * BLOCKS + b]
            part = gathered[b * ROWS : (b + 1) * ROWS]
            query = jnp.concatenate([part[:, h * HD : (h + 1) * HD] for h in range(heads)], axis=0)
            new_key = jnp.concatenate([part[:, heads * HD : (heads + 1) * HD]] * heads, axis=0)
            new_value = jnp.concatenate([part[:, (heads + 1) * HD :]] * heads, axis=0)
            past = dot_nt(query, keys[ancestor]) * scale
            own = jnp.sum(query.astype(F32) * new_key.astype(F32), axis=1, keepdims=True) * scale
            top = jnp.maximum(jnp.max(past, axis=1, keepdims=True), own)
            weight = jnp.exp(past - top)
            own = jnp.exp(own - top)
            norm = jnp.sum(weight, axis=1, keepdims=True) + own
            mix = dot(weight.astype(BF16), values[ancestor])
            mix = mix + own.astype(BF16).astype(F32) * new_value.astype(F32)
            mix = (mix / norm).astype(BF16)
            results.append(
                jnp.concatenate([mix[h * ROWS : (h + 1) * ROWS] for h in range(heads)], axis=1)
            )
        total[...] += dot(taken, jnp.concatenate(results, axis=0))
        return carry

    lax.fori_loop(0, steps, step, 0)
    out_ref[...] = total[...].astype(BF16)


def project_kernel(cross, rows_ref, *refs):
    x = lax.axis_index("x")
    for j in range(cross):
        refs[-1][lax.rem(x + j, cross)] = dot(rows_ref[...], refs[j][...]).astype(BF16)


def ring(n, by):
    return [(i, (i + by) % n) for i in range(n)]


def on_device(queries, new_keys, new_values, cache_keys, cache_values, ancestors, out_weight):
    lines = lax.axis_size("z")
    cross = lax.axis_size("x")
    groups = lines * cross
    members = cache_keys.shape[0]
    span = cross * members
    width = queries.shape[1]
    columns = out_weight.shape[1]
    everything = width + 2 * HD

    weights = [out_weight] + [lax.ppermute(out_weight, "x", ring(cross, cross - by)) for by in range(1, cross)]

    sent, own, tables, need = call(
        functools.partial(prepare_kernel, cross),
        "prepare",
        out=[
            jax.ShapeDtypeStruct((groups * FIRST, everything), BF16),
            jax.ShapeDtypeStruct((16, LANES), jnp.int32),
            jax.ShapeDtypeStruct((groups, 2 * LANES), BF16),
            jax.ShapeDtypeStruct((1,), jnp.int32),
        ],
        n_vmem=4,
        out_specs=[pl.BlockSpec(memory_space=VMEM)] * 3 + [pl.BlockSpec(memory_space=pltpu.SMEM)],
    )(ancestors.reshape(lines, span), queries, new_keys, new_values)

    def exchange(cap):
        packed = sent
        if cap != FIRST:
            packed = call(
                functools.partial(pack_kernel, cap),
                "pack",
                out=jax.ShapeDtypeStruct((groups * cap, everything), BF16),
                n_vmem=4,
            )(own, queries, new_keys, new_values)
        received = lax.all_to_all(packed.reshape(groups, cap, everything), DOM, 0, 0, tiled=True)
        mixed = call(
            functools.partial(attend_kernel, cap, cross),
            "attend",
            out=jax.ShapeDtypeStruct((groups * cap, width), BF16),
            n_vmem=2,
            n_any=2,
            scratch=[
                pltpu.VMEM(cache_keys.shape, BF16),
                pltpu.VMEM(cache_values.shape, BF16),
                pltpu.VMEM((8, LANES), jnp.int32),
                pltpu.SMEM((8, LANES), jnp.int32),
                pltpu.VMEM((groups * cap, width), F32),
                pltpu.SemaphoreType.DMA((2,)),
                pltpu.SemaphoreType.DMA,
            ],
            limit=40,
        )(tables, received.reshape(groups * cap, everything), cache_keys, cache_values)
        returned = lax.all_to_all(mixed.reshape(groups, cap, width), DOM, 0, 0, tiled=True)
        return call(
            functools.partial(unpack_kernel, cap),
            "unpack",
            out=jax.ShapeDtypeStruct((lines, members, width), BF16),
            n_vmem=2,
        )(own, returned.reshape(groups * cap, width))

    level = jnp.where(need[0] <= FIRST, 0, jnp.where(need[0] <= 2 * FIRST, 1, 2))
    heads_out = lax.switch(level, [functools.partial(exchange, c) for c in (FIRST, 2 * FIRST, members)])

    heads_out, *weights = lax.optimization_barrier((heads_out, *weights))
    column = lax.all_to_all(heads_out, "z", 0, 0, tiled=True).reshape(lines * members, width)
    partial_rows = call(
        functools.partial(project_kernel, cross),
        "project",
        out=jax.ShapeDtypeStruct((cross, lines * members, columns), BF16),
        n_vmem=1 + cross,
    )(column, *weights)
    shares = lax.all_to_all(
        partial_rows.reshape(cross * lines, members, columns), ("x",) + TP, 0, 0, tiled=True
    )
    summed = jnp.sum(shares.reshape(cross, lines, members, columns).astype(F32), axis=1)
    return summed.reshape(cross * members, columns).astype(BF16)


def solution(mesh):
    inner = Mesh(mesh.devices.reshape(8, 4, 4, 2), DOM + TP)
    return jax.shard_map(
        on_device,
        mesh=inner,
        in_specs=(P(DOM, TP), P(DOM, TP), P(DOM, TP), P(DOM, None, TP), P(DOM, None, TP), P(), P(TP, DOM)),
        out_specs=P(TP, DOM),
        check_vma=False,
    )
```

```python
import functools
import math

import jax
import jax.numpy as jnp
from jax import lax
from jax.experimental import pallas as pl
from jax.experimental.pallas import tpu as pltpu
from jax.sharding import Mesh, PartitionSpec as P

HD = 128
ROWS = 16
BLOCKS = 8
LANES = 128
FIRST = 8
VMEM = pltpu.VMEM
F32 = jnp.float32
BF16 = jnp.bfloat16
DOM = ("z", "x")
TP = ("y", "core")


def iota(shape, dim):
    return lax.broadcasted_iota(jnp.int32, shape, dim)


def dot(a, b):
    return jnp.dot(a, b, preferred_element_type=F32)


def dot_tn(a, b):
    return lax.dot_general(a, b, (((0,), (0,)), ((), ())), preferred_element_type=F32)


def dot_nt(a, b):
    return lax.dot_general(a, b, (((1,), (1,)), ((), ())), preferred_element_type=F32)


def call(body, name, *, out, n_vmem, n_any=0, scratch=(), limit=24, out_specs=None):
    return pl.pallas_call(
        body,
        out_shape=out,
        in_specs=[pl.BlockSpec(memory_space=VMEM)] * n_vmem + [pl.BlockSpec(memory_space=pl.ANY)] * n_any,
        out_specs=out_specs or pl.BlockSpec(memory_space=VMEM),
        scratch_shapes=scratch,
        compiler_params=pltpu.CompilerParams(vmem_limit_bytes=limit << 20),
        name=name,
    )


def whole(cap):
    return cap // 8 * 8


def lanes(cap, width):
    return width + (width // 2 if cap % 8 else 0)


def picks(own_ref, cap, slots, members):
    rows = whole(cap)
    source, slot = own_ref[0:1, :members], own_ref[8:9, :members]
    index = iota((slots, members), 0)
    pick = ((index == source * rows + slot) & (slot < rows)).astype(BF16)
    if cap == rows:
        return pick, None, None
    left = (index == source * rows + slot - rows) & (slot >= rows)
    right = (index == source * rows + slot - rows + 4) & (slot >= rows)
    return pick, left.astype(BF16), right.astype(BF16)


def fill(own_ref, cap, q_ref, k_ref, v_ref, out_ref):
    width = q_ref.shape[1]
    pick, left, right = picks(own_ref, cap, out_ref.shape[0], q_ref.shape[0])
    out_ref[:, :width] = dot(pick, q_ref[...]).astype(BF16)
    out_ref[:, width : width + HD] = dot(pick, k_ref[...]).astype(BF16)
    out_ref[:, width + HD : width + 2 * HD] = dot(pick, v_ref[...]).astype(BF16)
    if left is not None:
        base = width + 2 * HD
        half = base // 2
        last = dot(right, jnp.concatenate([q_ref[:, half:], k_ref[...], v_ref[...]], axis=1))
        out_ref[:, base:] = (dot(left, q_ref[:, :half]) + last).astype(BF16)


def prepare_kernel(cross, anc_ref, q_ref, k_ref, v_ref, sent_ref, own_ref, tables_ref, need_ref):
    lines = anc_ref.shape[0]
    members = q_ref.shape[0]
    groups = lines * cross
    z, x = lax.axis_index("z"), lax.axis_index("x")
    anc = jnp.concatenate(
        [anc_ref[...]] + [pltpu.roll(anc_ref[...], LANES - members * j, 1) for j in range(1, cross)], axis=0
    )
    inside = iota((groups, LANES), 1) < members
    source = jnp.where(inside, anc // members, -1)
    local = anc % members
    lane = iota((groups, LANES), 1)
    slot = jnp.zeros((groups, LANES), jnp.int32)
    for k in range(1, members):
        slot += ((source == pltpu.roll(source, k, 1)) & (lane >= k)).astype(jnp.int32)
    slot = jnp.where(inside, slot, 0)
    need_ref[0] = jnp.max(slot) + 1
    mine = source == z * cross + x
    tables_ref[:, :LANES] = jnp.where(mine, slot, -1).astype(F32).astype(BF16)
    tables_ref[:, LANES:] = jnp.where(mine, local, 0).astype(F32).astype(BF16)
    here = iota((groups, LANES), 0) == x * lines + z
    own_ref[0:8] = jnp.broadcast_to(jnp.sum(jnp.where(here, source, 0), axis=0, keepdims=True), (8, LANES))
    own_ref[8:16] = jnp.broadcast_to(jnp.sum(jnp.where(here, slot, 0), axis=0, keepdims=True), (8, LANES))
    fill(own_ref, FIRST, q_ref, k_ref, v_ref, sent_ref)


def pack_kernel(cap, own_ref, q_ref, k_ref, v_ref, sent_ref):
    fill(own_ref, cap, q_ref, k_ref, v_ref, sent_ref)


def unpack_kernel(cap, own_ref, returned_ref, out_ref):
    members = out_ref.shape[-2]
    width = out_ref.shape[-1]
    pick, left, right = picks(own_ref, cap, returned_ref.shape[0], members)
    rows = dot_tn(pick, returned_ref[:, :width])
    if left is not None:
        halves = returned_ref[:, width:]
        rows += jnp.concatenate([dot_tn(left, halves), dot_tn(right, halves)], axis=1)
    rows = rows.astype(BF16)
    for i in range(out_ref.shape[0]):
        out_ref[i] = rows


def attend_kernel(
    cap, cross, tables_ref, recv_ref, keys_ref, values_ref, out_ref,
    keys, values, order, order_smem, total, sems, order_sem,
):
    load_keys = pltpu.make_async_copy(keys_ref, keys, sems.at[0])
    load_values = pltpu.make_async_copy(values_ref, values, sems.at[1])
    load_keys.start()
    load_values.start()
    deep = whole(cap)
    base_rows = recv_ref.shape[0]
    rows = base_rows if cap == deep else 2 * base_rows
    groups = tables_ref.shape[0]
    lines = groups // cross
    width = total.shape[1] if cap == deep else total.shape[1] // 3 * 2
    heads = width // HD
    everything = width + 2 * HD
    scale = 1.0 / math.sqrt(HD)

    group = iota((rows, groups), 0) % base_rows // deep
    repeat = ((group % cross) * lines + group // cross == iota((rows, groups), 1)).astype(BF16)
    spread = dot(repeat, tables_ref[...])
    index = iota((rows, LANES), 0)
    slot = index % deep
    if cap != deep:
        slot = jnp.where(index < base_rows, slot, jnp.where(slot < 4, slot + deep, -2))
    hit = spread[:, :LANES] == slot.astype(F32)
    local = jnp.sum(jnp.where(hit, spread[:, LANES:] + 1.0, 0.0), axis=1, keepdims=True) - 1.0

    member = (local == iota((rows, LANES), 1).astype(F32)).astype(F32)
    before = (iota((rows, rows), 1) < iota((rows, rows), 0)).astype(BF16)
    rank = dot(before, member.astype(BF16))
    count = jnp.sum(member, axis=0, keepdims=True)
    blocks = jnp.floor((count + (ROWS - 1)) * (1.0 / ROWS))
    upto = (iota((LANES, LANES), 0) < iota((LANES, LANES), 1)).astype(BF16)
    first = dot(jnp.broadcast_to(blocks, (8, LANES)).astype(BF16), upto)[0:1]
    position = jnp.sum(member * (rank + first * ROWS), axis=1, keepdims=True)
    position = jnp.where(local >= 0.0, position, -1.0)
    position_row = jnp.transpose(jnp.broadcast_to(position, (rows, LANES)))[0:1]
    steps = (jnp.sum(blocks).astype(jnp.int32) + BLOCKS - 1) // BLOCKS
    ended = (first + blocks) <= iota((LANES, LANES), 0).astype(F32)
    owner = jnp.sum(jnp.where(ended & (iota((LANES, LANES), 1) < groups), 1.0, 0.0), axis=1, keepdims=True)
    owner = jnp.minimum(owner, groups - 1.0)
    order[...] = jnp.transpose(jnp.broadcast_to(owner, (LANES, LANES)))[0:8].astype(jnp.int32)
    move = pltpu.make_async_copy(order, order_smem, order_sem)
    move.start()
    total[...] = jnp.zeros_like(total)
    move.wait()
    load_keys.wait()
    load_values.wait()

    def step(k, carry):
        base = (k * (BLOCKS * ROWS)).astype(F32)
        taken = (position - base == iota((rows, BLOCKS * ROWS), 1).astype(F32)).astype(BF16)
        across = (position_row - base == iota((BLOCKS * ROWS, rows), 0).astype(F32)).astype(BF16)
        gathered = dot(across[:, :base_rows], recv_ref[:, :everything])
        if cap != deep:
            left = taken[base_rows:]
            right = pltpu.roll(left.astype(F32), 4, 0).astype(BF16)
            halves = recv_ref[:, everything:]
            gathered += jnp.concatenate([dot_tn(left, halves), dot_tn(right, halves)], axis=1)
        gathered = gathered.astype(BF16)
        results = []
        for b in range(BLOCKS):
            ancestor = order_smem[0, k * BLOCKS + b]
            part = gathered[b * ROWS : (b + 1) * ROWS]
            query = jnp.concatenate([part[:, h * HD : (h + 1) * HD] for h in range(heads)], axis=0)
            new_key = jnp.concatenate([part[:, heads * HD : (heads + 1) * HD]] * heads, axis=0)
            new_value = jnp.concatenate([part[:, (heads + 1) * HD :]] * heads, axis=0)
            past = dot_nt(query, keys[ancestor]) * scale
            own = jnp.sum(query.astype(F32) * new_key.astype(F32), axis=1, keepdims=True) * scale
            top = jnp.maximum(jnp.max(past, axis=1, keepdims=True), own)
            weight = jnp.exp(past - top)
            own = jnp.exp(own - top)
            norm = jnp.sum(weight, axis=1, keepdims=True) + own
            mix = dot(weight.astype(BF16), values[ancestor])
            mix = mix + own.astype(BF16).astype(F32) * new_value.astype(F32)
            mix = (mix / norm).astype(BF16)
            results.append(
                jnp.concatenate([mix[h * ROWS : (h + 1) * ROWS] for h in range(heads)], axis=1)
            )
        result = jnp.concatenate(results, axis=0)
        total[:, :width] += dot(taken[:base_rows], result)
        if cap != deep:
            total[:, width:] += dot(left, result[:, : width // 2]) + dot(right, result[:, width // 2 :])
        return carry

    lax.fori_loop(0, steps, step, 0)
    out_ref[...] = total[...].astype(BF16)


def project_kernel(cross, rows_ref, *refs):
    x = lax.axis_index("x")
    for j in range(cross):
        refs[-1][lax.rem(x + j, cross)] = dot(rows_ref[...], refs[j][...]).astype(BF16)


def ring(n, by):
    return [(i, (i + by) % n) for i in range(n)]


def on_device(queries, new_keys, new_values, cache_keys, cache_values, ancestors, out_weight):
    lines = lax.axis_size("z")
    cross = lax.axis_size("x")
    groups = lines * cross
    members = cache_keys.shape[0]
    span = cross * members
    width = queries.shape[1]
    columns = out_weight.shape[1]
    everything = width + 2 * HD

    weights = [out_weight] + [lax.ppermute(out_weight, "x", ring(cross, cross - by)) for by in range(1, cross)]

    sent, own, tables, need = call(
        functools.partial(prepare_kernel, cross),
        "prepare",
        out=[
            jax.ShapeDtypeStruct((groups * FIRST, everything), BF16),
            jax.ShapeDtypeStruct((16, LANES), jnp.int32),
            jax.ShapeDtypeStruct((groups, 2 * LANES), BF16),
            jax.ShapeDtypeStruct((1,), jnp.int32),
        ],
        n_vmem=4,
        out_specs=[pl.BlockSpec(memory_space=VMEM)] * 3 + [pl.BlockSpec(memory_space=pltpu.SMEM)],
    )(ancestors.reshape(lines, span), queries, new_keys, new_values)

    def exchange(cap):
        rows = whole(cap)
        packed = sent
        if cap != FIRST:
            packed = call(
                functools.partial(pack_kernel, cap),
                "pack",
                out=jax.ShapeDtypeStruct((groups * rows, lanes(cap, everything)), BF16),
                n_vmem=4,
            )(own, queries, new_keys, new_values)
        received = lax.all_to_all(packed.reshape(groups, rows, -1), DOM, 0, 0, tiled=True)
        mixed = call(
            functools.partial(attend_kernel, cap, cross),
            "attend",
            out=jax.ShapeDtypeStruct((groups * rows, lanes(cap, width)), BF16),
            n_vmem=2,
            n_any=2,
            scratch=[
                pltpu.VMEM(cache_keys.shape, BF16),
                pltpu.VMEM(cache_values.shape, BF16),
                pltpu.VMEM((8, LANES), jnp.int32),
                pltpu.SMEM((8, LANES), jnp.int32),
                pltpu.VMEM((groups * rows, lanes(cap, width)), F32),
                pltpu.SemaphoreType.DMA((2,)),
                pltpu.SemaphoreType.DMA,
            ],
            limit=40,
        )(tables, received.reshape(groups * rows, -1), cache_keys, cache_values)
        returned = lax.all_to_all(mixed.reshape(groups, rows, -1), DOM, 0, 0, tiled=True)
        return call(
            functools.partial(unpack_kernel, cap),
            "unpack",
            out=jax.ShapeDtypeStruct((lines, members, width), BF16),
            n_vmem=2,
        )(own, returned.reshape(groups * rows, -1))

    caps = (FIRST, 12, 16, members)
    level = sum((need[0] > c).astype(jnp.int32) for c in caps[:-1])
    heads_out = lax.switch(level, [functools.partial(exchange, c) for c in caps])

    heads_out, *weights = lax.optimization_barrier((heads_out, *weights))
    column = lax.all_to_all(heads_out, "z", 0, 0, tiled=True).reshape(lines * members, width)
    partial_rows = call(
        functools.partial(project_kernel, cross),
        "project",
        out=jax.ShapeDtypeStruct((cross, lines * members, columns), BF16),
        n_vmem=1 + cross,
    )(column, *weights)
    shares = lax.all_to_all(
        partial_rows.reshape(cross * lines, members, columns), ("x",) + TP, 0, 0, tiled=True
    )
    summed = jnp.sum(shares.reshape(cross, lines, members, columns).astype(F32), axis=1)
    return summed.reshape(cross * members, columns).astype(BF16)


def solution(mesh):
    inner = Mesh(mesh.devices.reshape(8, 4, 4, 2), DOM + TP)
    return jax.shard_map(
        on_device,
        mesh=inner,
        in_specs=(P(DOM, TP), P(DOM, TP), P(DOM, TP), P(DOM, None, TP), P(DOM, None, TP), P(), P(TP, DOM)),
        out_specs=P(TP, DOM),
        check_vma=False,
    )
```

```python
import functools
import math

import jax
import jax.numpy as jnp
from jax import lax
from jax.experimental import pallas as pl
from jax.experimental.pallas import tpu as pltpu
from jax.sharding import Mesh, PartitionSpec as P

HD = 128
ROWS = 16
BLOCKS = 12
LANES = 128
FIRST = 8
VMEM = pltpu.VMEM
F32 = jnp.float32
BF16 = jnp.bfloat16
DOM = ("z", "x")
TP = ("y", "core")


def iota(shape, dim):
    return lax.broadcasted_iota(jnp.int32, shape, dim)


def dot(a, b):
    return jnp.dot(a, b, preferred_element_type=F32)


def dot_tn(a, b):
    return lax.dot_general(a, b, (((0,), (0,)), ((), ())), preferred_element_type=F32)


def dot_nt(a, b):
    return lax.dot_general(a, b, (((1,), (1,)), ((), ())), preferred_element_type=F32)


def call(body, name, *, out, n_vmem, n_any=0, scratch=(), limit=24, out_specs=None):
    return pl.pallas_call(
        body,
        out_shape=out,
        in_specs=[pl.BlockSpec(memory_space=VMEM)] * n_vmem + [pl.BlockSpec(memory_space=pl.ANY)] * n_any,
        out_specs=out_specs or pl.BlockSpec(memory_space=VMEM),
        scratch_shapes=scratch,
        compiler_params=pltpu.CompilerParams(vmem_limit_bytes=limit << 20),
        name=name,
    )


def whole(cap):
    return cap // 8 * 8


def lanes(cap, width):
    return width + (width // 2 if cap % 8 else 0)


def picks(own_ref, cap, slots, members):
    rows = whole(cap)
    source, slot = own_ref[0:1, :members], own_ref[8:9, :members]
    index = iota((slots, members), 0)
    pick = ((index == source * rows + slot) & (slot < rows)).astype(BF16)
    if cap == rows:
        return pick, None, None
    left = (index == source * rows + slot - rows) & (slot >= rows)
    right = (index == source * rows + slot - rows + 4) & (slot >= rows)
    return pick, left.astype(BF16), right.astype(BF16)


def fill(own_ref, cap, q_ref, k_ref, v_ref, out_ref):
    width = q_ref.shape[1]
    pick, left, right = picks(own_ref, cap, out_ref.shape[0], q_ref.shape[0])
    out_ref[:, :width] = dot(pick, q_ref[...]).astype(BF16)
    out_ref[:, width : width + HD] = dot(pick, k_ref[...]).astype(BF16)
    out_ref[:, width + HD : width + 2 * HD] = dot(pick, v_ref[...]).astype(BF16)
    if left is not None:
        base = width + 2 * HD
        half = base // 2
        last = dot(right, jnp.concatenate([q_ref[:, half:], k_ref[...], v_ref[...]], axis=1))
        out_ref[:, base:] = (dot(left, q_ref[:, :half]) + last).astype(BF16)


def prepare_kernel(cross, caps, anc_ref, q_ref, k_ref, v_ref, sent_ref, own_ref, tables_ref, level_ref):
    lines = anc_ref.shape[0]
    members = q_ref.shape[0]
    groups = lines * cross
    z, x = lax.axis_index("z"), lax.axis_index("x")
    anc = anc_ref[...]
    source = anc // members
    place = iota(anc.shape, 1) % members
    slot = jnp.zeros(anc.shape, jnp.int32)
    for k in range(1, members):
        slot += ((source == pltpu.roll(source, k, 1)) & (place >= k)).astype(jnp.int32)
    need = jnp.max(slot) + 1
    level_ref[0] = sum((need > c).astype(jnp.int32) for c in caps[:-1])
    inside = iota((groups, LANES), 1) < members

    def by_group(a):
        turns = [a] + [pltpu.roll(a, LANES - members * j, 1) for j in range(1, cross)]
        return jnp.where(inside, jnp.concatenate(turns, axis=0), -1)

    source, local, slot = by_group(source), by_group(anc % members), by_group(slot)
    mine = source == z * cross + x
    tables_ref[:, :LANES] = jnp.where(mine, slot, -1).astype(F32).astype(BF16)
    tables_ref[:, LANES:] = local.astype(F32).astype(BF16)
    here = iota((groups, LANES), 0) == x * lines + z
    own_ref[0:8] = jnp.broadcast_to(jnp.sum(jnp.where(here, source, 0), axis=0, keepdims=True), (8, LANES))
    own_ref[8:16] = jnp.broadcast_to(jnp.sum(jnp.where(here, slot, 0), axis=0, keepdims=True), (8, LANES))
    fill(own_ref, FIRST, q_ref, k_ref, v_ref, sent_ref)


def pack_kernel(cap, own_ref, q_ref, k_ref, v_ref, sent_ref):
    fill(own_ref, cap, q_ref, k_ref, v_ref, sent_ref)


def unpack_kernel(cap, own_ref, returned_ref, out_ref):
    members = out_ref.shape[-2]
    width = out_ref.shape[-1]
    pick, left, right = picks(own_ref, cap, returned_ref.shape[0], members)
    rows = dot_tn(pick, returned_ref[:, :width])
    if left is not None:
        halves = returned_ref[:, width:]
        rows += jnp.concatenate([dot_tn(left, halves), dot_tn(right, halves)], axis=1)
    rows = rows.astype(BF16)
    for i in range(out_ref.shape[0]):
        out_ref[i] = rows


def attend_kernel(
    cap, cross, tables_ref, recv_ref, keys_ref, values_ref, out_ref,
    keys, values, order, order_smem, total, sems, order_sem,
):
    load_keys = pltpu.make_async_copy(keys_ref, keys, sems.at[0])
    load_values = pltpu.make_async_copy(values_ref, values, sems.at[1])
    load_keys.start()
    load_values.start()
    deep = whole(cap)
    base_rows = recv_ref.shape[0]
    rows = base_rows if cap == deep else 2 * base_rows
    groups = tables_ref.shape[0]
    lines = groups // cross
    width = total.shape[1] if cap == deep else total.shape[1] // 3 * 2
    heads = width // HD
    everything = width + 2 * HD
    scale = 1.0 / math.sqrt(HD)

    group = iota((rows, groups), 0) % base_rows // deep
    repeat = ((group % cross) * lines + group // cross == iota((rows, groups), 1)).astype(BF16)
    spread = dot(repeat, tables_ref[...])
    index = iota((rows, LANES), 0)
    slot = index % deep
    if cap != deep:
        slot = jnp.where(index < base_rows, slot, jnp.where(slot < 4, slot + deep, -2))
    hit = spread[:, :LANES] == slot.astype(F32)
    local = jnp.sum(jnp.where(hit, spread[:, LANES:] + 1.0, 0.0), axis=1, keepdims=True) - 1.0

    member = (local == iota((rows, LANES), 1).astype(F32)).astype(F32)
    before = (iota((rows, rows), 1) < iota((rows, rows), 0)).astype(BF16)
    rank = dot(before, member.astype(BF16))
    count = jnp.sum(member, axis=0, keepdims=True)
    blocks = jnp.floor((count + (ROWS - 1)) * (1.0 / ROWS))
    upto = (iota((LANES, LANES), 0) < iota((LANES, LANES), 1)).astype(BF16)
    first = dot(jnp.broadcast_to(blocks, (8, LANES)).astype(BF16), upto)[0:1]
    position = jnp.sum(member * (rank + first * ROWS), axis=1, keepdims=True)
    position = jnp.where(local >= 0.0, position, -1.0)
    position_row = jnp.transpose(jnp.broadcast_to(position, (rows, LANES)))[0:1]
    steps = (jnp.sum(blocks).astype(jnp.int32) + BLOCKS - 1) // BLOCKS
    ended = (first + blocks) <= iota((LANES, LANES), 0).astype(F32)
    owner = jnp.sum(jnp.where(ended & (iota((LANES, LANES), 1) < groups), 1.0, 0.0), axis=1, keepdims=True)
    owner = jnp.minimum(owner, groups - 1.0)
    order[...] = jnp.transpose(jnp.broadcast_to(owner, (LANES, LANES)))[0:8].astype(jnp.int32)
    move = pltpu.make_async_copy(order, order_smem, order_sem)
    move.start()
    total[...] = jnp.zeros_like(total)
    move.wait()
    load_keys.wait()
    load_values.wait()

    def step(k, carry):
        base = (k * (BLOCKS * ROWS)).astype(F32)
        taken = (position - base == iota((rows, BLOCKS * ROWS), 1).astype(F32)).astype(BF16)
        across = (position_row - base == iota((BLOCKS * ROWS, rows), 0).astype(F32)).astype(BF16)
        gathered = dot(across[:, :base_rows], recv_ref[:, :everything])
        if cap != deep:
            left = taken[base_rows:]
            right = pltpu.roll(left.astype(F32), 4, 0).astype(BF16)
            halves = recv_ref[:, everything:]
            gathered += jnp.concatenate([dot_tn(left, halves), dot_tn(right, halves)], axis=1)
        gathered = gathered.astype(BF16)
        results = []
        for b in range(BLOCKS):
            ancestor = order_smem[0, k * BLOCKS + b]
            part = gathered[b * ROWS : (b + 1) * ROWS]
            query = jnp.concatenate([part[:, h * HD : (h + 1) * HD] for h in range(heads)], axis=0)
            new_key = jnp.concatenate([part[:, heads * HD : (heads + 1) * HD]] * heads, axis=0)
            new_value = jnp.concatenate([part[:, (heads + 1) * HD :]] * heads, axis=0)
            past = dot_nt(query, keys[ancestor]) * scale
            own = jnp.sum(query.astype(F32) * new_key.astype(F32), axis=1, keepdims=True) * scale
            top = jnp.maximum(jnp.max(past, axis=1, keepdims=True), own)
            weight = jnp.exp(past - top)
            own = jnp.exp(own - top)
            norm = jnp.sum(weight, axis=1, keepdims=True) + own
            mix = dot(weight.astype(BF16), values[ancestor])
            mix = mix + own.astype(BF16).astype(F32) * new_value.astype(F32)
            mix = (mix / norm).astype(BF16)
            results.append(
                jnp.concatenate([mix[h * ROWS : (h + 1) * ROWS] for h in range(heads)], axis=1)
            )
        result = jnp.concatenate(results, axis=0)
        total[:, :width] += dot(taken[:base_rows], result)
        if cap != deep:
            total[:, width:] += dot(left, result[:, : width // 2]) + dot(right, result[:, width // 2 :])
        return carry

    lax.fori_loop(0, steps, step, 0)
    out_ref[...] = total[...].astype(BF16)


def project_kernel(cross, rows_ref, *refs):
    x = lax.axis_index("x")
    for j in range(cross):
        refs[-1][lax.rem(x + j, cross)] = dot(rows_ref[...], refs[j][...]).astype(BF16)


def ring(n, by):
    return [(i, (i + by) % n) for i in range(n)]


def on_device(queries, new_keys, new_values, cache_keys, cache_values, ancestors, out_weight):
    lines = lax.axis_size("z")
    cross = lax.axis_size("x")
    groups = lines * cross
    members = cache_keys.shape[0]
    span = cross * members
    width = queries.shape[1]
    columns = out_weight.shape[1]
    everything = width + 2 * HD

    weights = [out_weight] + [lax.ppermute(out_weight, "x", ring(cross, cross - by)) for by in (1, cross - 1)]

    caps = (FIRST, 12, 16, members)
    sent, own, tables, level = call(
        functools.partial(prepare_kernel, cross, caps),
        "prepare",
        out=[
            jax.ShapeDtypeStruct((groups * FIRST, everything), BF16),
            jax.ShapeDtypeStruct((16, LANES), jnp.int32),
            jax.ShapeDtypeStruct((groups, 2 * LANES), BF16),
            jax.ShapeDtypeStruct((1,), jnp.int32),
        ],
        n_vmem=4,
        out_specs=[pl.BlockSpec(memory_space=VMEM)] * 3 + [pl.BlockSpec(memory_space=pltpu.SMEM)],
    )(ancestors.reshape(lines, span), queries, new_keys, new_values)

    def exchange(cap):
        rows = whole(cap)
        packed = sent
        if cap != FIRST:
            packed = call(
                functools.partial(pack_kernel, cap),
                "pack",
                out=jax.ShapeDtypeStruct((groups * rows, lanes(cap, everything)), BF16),
                n_vmem=4,
            )(own, queries, new_keys, new_values)
        received = lax.all_to_all(packed.reshape(groups, rows, -1), DOM, 0, 0, tiled=True)
        mixed = call(
            functools.partial(attend_kernel, cap, cross),
            "attend",
            out=jax.ShapeDtypeStruct((groups * rows, lanes(cap, width)), BF16),
            n_vmem=2,
            n_any=2,
            scratch=[
                pltpu.VMEM(cache_keys.shape, BF16),
                pltpu.VMEM(cache_values.shape, BF16),
                pltpu.VMEM((8, LANES), jnp.int32),
                pltpu.SMEM((8, LANES), jnp.int32),
                pltpu.VMEM((groups * rows, lanes(cap, width)), F32),
                pltpu.SemaphoreType.DMA((2,)),
                pltpu.SemaphoreType.DMA,
            ],
            limit=40,
        )(tables, received.reshape(groups * rows, -1), cache_keys, cache_values)
        returned = lax.all_to_all(mixed.reshape(groups, rows, -1), DOM, 0, 0, tiled=True)
        return call(
            functools.partial(unpack_kernel, cap),
            "unpack",
            out=jax.ShapeDtypeStruct((lines, members, width), BF16),
            n_vmem=2,
        )(own, returned.reshape(groups * rows, -1))

    heads_out = lax.switch(level[0], [functools.partial(exchange, c) for c in caps])

    heads_out, *weights = lax.optimization_barrier((heads_out, *weights))
    weights.insert(2, lax.ppermute(weights[1], "x", ring(cross, cross - 1)))
    column = lax.all_to_all(heads_out, "z", 0, 0, tiled=True).reshape(lines * members, width)
    partial_rows = call(
        functools.partial(project_kernel, cross),
        "project",
        out=jax.ShapeDtypeStruct((cross, lines * members, columns), BF16),
        n_vmem=1 + cross,
    )(column, *weights)
    shares = lax.all_to_all(
        partial_rows.reshape(cross * lines, members, columns), ("x",) + TP, 0, 0, tiled=True
    )
    summed = jnp.sum(shares.reshape(cross, lines, members, columns).astype(F32), axis=1)
    return summed.reshape(cross * members, columns).astype(BF16)


def solution(mesh):
    inner = Mesh(mesh.devices.reshape(8, 4, 4, 2), DOM + TP)
    return jax.shard_map(
        on_device,
        mesh=inner,
        in_specs=(P(DOM, TP), P(DOM, TP), P(DOM, TP), P(DOM, None, TP), P(DOM, None, TP), P(), P(TP, DOM)),
        out_specs=P(TP, DOM),
        check_vma=False,
    )
```

```python
import functools
import math

import jax
import jax.numpy as jnp
from jax import lax
from jax.experimental import pallas as pl
from jax.experimental.pallas import tpu as pltpu
from jax.sharding import Mesh, PartitionSpec as P

HD = 128
ROWS = 16
BLOCKS = 12
LANES = 128
FIRST = 8
VMEM = pltpu.VMEM
F32 = jnp.float32
BF16 = jnp.bfloat16
DOM = ("z", "x")
TP = ("y", "core")


def iota(shape, dim):
    return lax.broadcasted_iota(jnp.int32, shape, dim)


def dot(a, b):
    return jnp.dot(a, b, preferred_element_type=F32)


def dot_tn(a, b):
    return lax.dot_general(a, b, (((0,), (0,)), ((), ())), preferred_element_type=F32)


def dot_nt(a, b):
    return lax.dot_general(a, b, (((1,), (1,)), ((), ())), preferred_element_type=F32)


def call(body, name, *, out, n_vmem=0, n_hbm=0, scratch=(), limit=24, out_specs=None):
    spaces = [VMEM] * n_vmem + [pltpu.HBM] * n_hbm
    return pl.pallas_call(
        body,
        out_shape=out,
        in_specs=[pl.BlockSpec(memory_space=space) for space in spaces],
        out_specs=out_specs or pl.BlockSpec(memory_space=VMEM),
        scratch_shapes=scratch,
        compiler_params=pltpu.CompilerParams(vmem_limit_bytes=limit << 20),
        name=name,
    )


def whole(cap):
    return cap // 8 * 8


def part_starts(cap, width):
    extra = cap % 8
    if not extra:
        return (), 0
    size = -(-(width // HD) * extra // 8) * HD
    return tuple(range(0, width, size)), size


def lanes(cap, width):
    return width + part_starts(cap, width)[1]


def picks(own_ref, cap, slots, members, count):
    rows = whole(cap)
    source, slot = own_ref[0:1, :members], own_ref[8:9, :members]
    index = iota((slots, members), 0) - source * rows
    found = [(index == slot) & (slot < rows)]
    for part in range(count):
        found.append((index == slot - rows + part * (cap % 8)) & (slot >= rows))
    return [one.astype(BF16) for one in found]


def fill(own_ref, cap, q_ref, k_ref, v_ref, out_ref):
    base = q_ref.shape[1] + 2 * HD
    starts, size = part_starts(cap, base)
    given = jnp.concatenate([q_ref[...], k_ref[...], v_ref[...]], axis=1)
    pick, *parts = picks(own_ref, cap, out_ref.shape[0], q_ref.shape[0], len(starts))
    out_ref[:, :base] = dot(pick, given).astype(BF16)
    if parts:
        total = None
        for start, part in zip(starts, parts):
            piece = given[:, start : start + size]
            if piece.shape[1] < size:
                piece = jnp.concatenate([piece, jnp.zeros((piece.shape[0], size - piece.shape[1]), BF16)], axis=1)
            term = dot(part, piece)
            total = term if total is None else total + term
        out_ref[:, base:] = total.astype(BF16)


def prepare_kernel(cross, caps, *refs):
    given, (sent_ref, own_ref, tables_ref, level_ref), held, sems = refs[:4], refs[4:8], refs[8:12], refs[12]
    copies = [pltpu.make_async_copy(a, b, sems.at[i]) for i, (a, b) in enumerate(zip(given, held))]
    for copy in copies:
        copy.start()
    anc_ref, q_ref, k_ref, v_ref = held
    lines = anc_ref.shape[0]
    members = q_ref.shape[0]
    groups = lines * cross
    z, x = lax.axis_index("z"), lax.axis_index("x")
    copies[0].wait()
    anc = anc_ref[...]
    source = anc // members
    place = iota(anc.shape, 1) % members
    slot = jnp.zeros(anc.shape, jnp.int32)
    for k in range(1, members):
        slot += ((source == pltpu.roll(source, k, 1)) & (place >= k)).astype(jnp.int32)
    need = jnp.max(slot) + 1
    level_ref[0] = sum((need > c).astype(jnp.int32) for c in caps[:-1])
    inside = iota((groups, LANES), 1) < members

    def by_group(a):
        turns = [a] + [pltpu.roll(a, LANES - members * j, 1) for j in range(1, cross)]
        return jnp.where(inside, jnp.concatenate(turns, axis=0), -1)

    source, local, slot = by_group(source), by_group(anc % members), by_group(slot)
    mine = source == z * cross + x
    tables_ref[:, :LANES] = jnp.where(mine, slot, -1).astype(F32).astype(BF16)
    tables_ref[:, LANES:] = local.astype(F32).astype(BF16)
    here = iota((groups, LANES), 0) == x * lines + z
    own_ref[0:8] = jnp.broadcast_to(jnp.sum(jnp.where(here, source, 0), axis=0, keepdims=True), (8, LANES))
    own_ref[8:16] = jnp.broadcast_to(jnp.sum(jnp.where(here, slot, 0), axis=0, keepdims=True), (8, LANES))
    for copy in copies[1:]:
        copy.wait()
    fill(own_ref, FIRST, q_ref, k_ref, v_ref, sent_ref)


def pack_kernel(cap, own_ref, q_ref, k_ref, v_ref, sent_ref):
    fill(own_ref, cap, q_ref, k_ref, v_ref, sent_ref)


def unpack_kernel(cap, own_ref, returned_ref, out_ref):
    members = out_ref.shape[-2]
    width = out_ref.shape[-1]
    starts, _ = part_starts(cap, width)
    pick, *parts = picks(own_ref, cap, returned_ref.shape[0], members, len(starts))
    rows = dot_tn(pick, returned_ref[:, :width])
    if parts:
        rows += jnp.concatenate([dot_tn(part, returned_ref[:, width:]) for part in parts], axis=1)
    rows = rows.astype(BF16)
    for i in range(out_ref.shape[0]):
        out_ref[i] = rows


def attend_kernel(
    cap, cross, tables_ref, recv_ref, keys_ref, values_ref, out_ref,
    keys, values, order, order_smem, total, sems, order_sem,
):
    load_keys = pltpu.make_async_copy(keys_ref, keys, sems.at[0])
    load_values = pltpu.make_async_copy(values_ref, values, sems.at[1])
    load_keys.start()
    load_values.start()
    deep = whole(cap)
    base_rows = recv_ref.shape[0]
    rows = base_rows if cap == deep else 2 * base_rows
    groups = tables_ref.shape[0]
    lines = groups // cross
    extra = cap - deep
    width = total.shape[1] // (8 + extra) * 8
    heads = width // HD
    everything = width + 2 * HD
    scale = 1.0 / math.sqrt(HD)

    group = iota((rows, groups), 0) % base_rows // deep
    repeat = ((group % cross) * lines + group // cross == iota((rows, groups), 1)).astype(BF16)
    spread = dot(repeat, tables_ref[...])
    index = iota((rows, LANES), 0)
    slot = index % deep
    if cap != deep:
        slot = jnp.where(index < base_rows, slot, jnp.where(slot < extra, slot + deep, -2))
    hit = spread[:, :LANES] == slot.astype(F32)
    local = jnp.sum(jnp.where(hit, spread[:, LANES:] + 1.0, 0.0), axis=1, keepdims=True) - 1.0

    member = (local == iota((rows, LANES), 1).astype(F32)).astype(F32)
    before = (iota((rows, rows), 1) < iota((rows, rows), 0)).astype(BF16)
    rank = dot(before, member.astype(BF16))
    count = jnp.sum(member, axis=0, keepdims=True)
    blocks = jnp.floor((count + (ROWS - 1)) * (1.0 / ROWS))
    upto = (iota((LANES, LANES), 0) < iota((LANES, LANES), 1)).astype(BF16)
    first = dot(jnp.broadcast_to(blocks, (8, LANES)).astype(BF16), upto)[0:1]
    position = jnp.sum(member * (rank + first * ROWS), axis=1, keepdims=True)
    position = jnp.where(local >= 0.0, position, -1.0)
    position_row = jnp.transpose(jnp.broadcast_to(position, (rows, LANES)))[0:1]
    steps = (jnp.sum(blocks).astype(jnp.int32) + BLOCKS - 1) // BLOCKS
    ended = (first + blocks) <= iota((LANES, LANES), 0).astype(F32)
    owner = jnp.sum(jnp.where(ended & (iota((LANES, LANES), 1) < groups), 1.0, 0.0), axis=1, keepdims=True)
    owner = jnp.minimum(owner, groups - 1.0)
    order[...] = jnp.transpose(jnp.broadcast_to(owner, (LANES, LANES)))[0:8].astype(jnp.int32)
    move = pltpu.make_async_copy(order, order_smem, order_sem)
    move.start()
    total[...] = jnp.zeros_like(total)
    move.wait()
    load_keys.wait()
    load_values.wait()

    def step(k, carry):
        base = (k * (BLOCKS * ROWS)).astype(F32)
        taken = (position - base == iota((rows, BLOCKS * ROWS), 1).astype(F32)).astype(BF16)
        across = (position_row - base == iota((BLOCKS * ROWS, rows), 0).astype(F32)).astype(BF16)
        gathered = dot(across[:, :base_rows], recv_ref[:, :everything])
        if cap != deep:
            starts, _ = part_starts(cap, everything)
            behind = across[:, base_rows:].astype(F32)
            pieces = [
                dot(pltpu.roll(behind, part * extra, 1).astype(BF16), recv_ref[:, everything:])
                for part in range(len(starts))
            ]
            gathered += jnp.concatenate(pieces, axis=1)[:, :everything]
        gathered = gathered.astype(BF16)
        results = []
        for b in range(BLOCKS):
            ancestor = order_smem[0, k * BLOCKS + b]
            part = gathered[b * ROWS : (b + 1) * ROWS]
            query = jnp.concatenate([part[:, h * HD : (h + 1) * HD] for h in range(heads)], axis=0)
            new_key = jnp.concatenate([part[:, heads * HD : (heads + 1) * HD]] * heads, axis=0)
            new_value = jnp.concatenate([part[:, (heads + 1) * HD :]] * heads, axis=0)
            past = dot_nt(query, keys[ancestor]) * scale
            own = jnp.sum(query.astype(F32) * new_key.astype(F32), axis=1, keepdims=True) * scale
            top = jnp.maximum(jnp.max(past, axis=1, keepdims=True), own)
            weight = jnp.exp(past - top)
            own = jnp.exp(own - top)
            norm = jnp.sum(weight, axis=1, keepdims=True) + own
            mix = dot(weight.astype(BF16), values[ancestor])
            mix = mix + own.astype(BF16).astype(F32) * new_value.astype(F32)
            mix = (mix / norm).astype(BF16)
            results.append(
                jnp.concatenate([mix[h * ROWS : (h + 1) * ROWS] for h in range(heads)], axis=1)
            )
        result = jnp.concatenate(results, axis=0)
        total[:, :width] += dot(taken[:base_rows], result)
        if cap != deep:
            starts, size = part_starts(cap, width)
            behind = taken[base_rows:].astype(F32)
            total[:, width:] += sum(
                dot(pltpu.roll(behind, part * extra, 0).astype(BF16), result[:, start : start + size])
                for part, start in enumerate(starts)
            )
        return carry

    lax.fori_loop(0, steps, step, 0)
    out_ref[...] = total[...].astype(BF16)


def project_kernel(cross, rows_ref, *refs):
    x = lax.axis_index("x")
    for j in range(cross):
        refs[-1][lax.rem(x + j, cross)] = dot(rows_ref[...], refs[j][...]).astype(BF16)


def ring(n, by):
    return [(i, (i + by) % n) for i in range(n)]


def on_device(queries, new_keys, new_values, cache_keys, cache_values, ancestors, out_weight):
    lines = lax.axis_size("z")
    cross = lax.axis_size("x")
    groups = lines * cross
    members = cache_keys.shape[0]
    span = cross * members
    width = queries.shape[1]
    columns = out_weight.shape[1]
    everything = width + 2 * HD

    weights = [out_weight] + [lax.ppermute(out_weight, "x", ring(cross, cross - by)) for by in (1, cross - 1)]

    caps = (FIRST, 9, 10, 12, 16, members)
    inputs = (ancestors.reshape(lines, span), queries, new_keys, new_values)
    sent, own, tables, level = call(
        functools.partial(prepare_kernel, cross, caps),
        "prepare",
        out=[
            jax.ShapeDtypeStruct((groups * FIRST, everything), BF16),
            jax.ShapeDtypeStruct((16, LANES), jnp.int32),
            jax.ShapeDtypeStruct((groups, 2 * LANES), BF16),
            jax.ShapeDtypeStruct((1,), jnp.int32),
        ],
        n_hbm=4,
        out_specs=[pl.BlockSpec(memory_space=VMEM)] * 3 + [pl.BlockSpec(memory_space=pltpu.SMEM)],
        scratch=[pltpu.VMEM(a.shape, a.dtype) for a in inputs] + [pltpu.SemaphoreType.DMA((4,))],
    )(*inputs)

    def exchange(cap):
        rows = whole(cap)
        packed = sent
        if cap != FIRST:
            packed = call(
                functools.partial(pack_kernel, cap),
                "pack",
                out=jax.ShapeDtypeStruct((groups * rows, lanes(cap, everything)), BF16),
                n_vmem=4,
            )(own, queries, new_keys, new_values)
        received = lax.all_to_all(packed.reshape(groups, rows, -1), DOM, 0, 0, tiled=True)
        mixed = call(
            functools.partial(attend_kernel, cap, cross),
            "attend",
            out=jax.ShapeDtypeStruct((groups * rows, lanes(cap, width)), BF16),
            n_vmem=2,
            n_hbm=2,
            scratch=[
                pltpu.VMEM(cache_keys.shape, BF16),
                pltpu.VMEM(cache_values.shape, BF16),
                pltpu.VMEM((8, LANES), jnp.int32),
                pltpu.SMEM((8, LANES), jnp.int32),
                pltpu.VMEM((groups * rows, lanes(cap, width)), F32),
                pltpu.SemaphoreType.DMA((2,)),
                pltpu.SemaphoreType.DMA,
            ],
            limit=40,
        )(tables, received.reshape(groups * rows, -1), cache_keys, cache_values)
        returned = lax.all_to_all(mixed.reshape(groups, rows, -1), DOM, 0, 0, tiled=True)
        return call(
            functools.partial(unpack_kernel, cap),
            "unpack",
            out=jax.ShapeDtypeStruct((lines, members, width), BF16),
            n_vmem=2,
        )(own, returned.reshape(groups * rows, -1))

    heads_out = lax.switch(level[0], [functools.partial(exchange, c) for c in caps])

    heads_out, *weights = lax.optimization_barrier((heads_out, *weights))
    weights.insert(2, lax.ppermute(weights[1], "x", ring(cross, cross - 1)))
    column = lax.all_to_all(heads_out, "z", 0, 0, tiled=True).reshape(lines * members, width)
    partial_rows = call(
        functools.partial(project_kernel, cross),
        "project",
        out=jax.ShapeDtypeStruct((cross, lines * members, columns), BF16),
        n_vmem=1 + cross,
    )(column, *weights)
    shares = lax.all_to_all(
        partial_rows.reshape(cross * lines, members, columns), ("x",) + TP, 0, 0, tiled=True
    )
    summed = jnp.sum(shares.reshape(cross, lines, members, columns).astype(F32), axis=1)
    return summed.reshape(cross * members, columns).astype(BF16)


def solution(mesh):
    inner = Mesh(mesh.devices.reshape(8, 4, 4, 2), DOM + TP)
    return jax.shard_map(
        on_device,
        mesh=inner,
        in_specs=(P(DOM, TP), P(DOM, TP), P(DOM, TP), P(DOM, None, TP), P(DOM, None, TP), P(), P(TP, DOM)),
        out_specs=P(TP, DOM),
        check_vma=False,
    )
```

```python
import functools
import math

import jax
import jax.numpy as jnp
from jax import lax
from jax.experimental import pallas as pl
from jax.experimental.pallas import tpu as pltpu
from jax.sharding import Mesh, PartitionSpec as P

HD = 128
ROWS = 16
BLOCKS = 11
LANES = 128
FIRST = 8
VMEM = pltpu.VMEM
F32 = jnp.float32
BF16 = jnp.bfloat16
DOM = ("z", "x")
TP = ("y", "core")


def iota(shape, dim):
    return lax.broadcasted_iota(jnp.int32, shape, dim)


def dot(a, b):
    return jnp.dot(a, b, preferred_element_type=F32)


def dot_tn(a, b):
    return lax.dot_general(a, b, (((0,), (0,)), ((), ())), preferred_element_type=F32)


def dot_nt(a, b):
    return lax.dot_general(a, b, (((1,), (1,)), ((), ())), preferred_element_type=F32)


def call(body, name, *, out, n_vmem=0, n_hbm=0, scratch=(), limit=24, out_specs=None):
    spaces = [VMEM] * n_vmem + [pltpu.HBM] * n_hbm
    return pl.pallas_call(
        body,
        out_shape=out,
        in_specs=[pl.BlockSpec(memory_space=space) for space in spaces],
        out_specs=out_specs or pl.BlockSpec(memory_space=VMEM),
        scratch_shapes=scratch,
        compiler_params=pltpu.CompilerParams(vmem_limit_bytes=limit << 20),
        name=name,
    )


def whole(cap):
    return cap // 8 * 8


def part_starts(cap, width):
    extra = cap % 8
    if not extra:
        return (), 0
    size = -(-(width // HD) * extra // 8) * HD
    return tuple(range(0, width, size)), size


def lanes(cap, width):
    return width + part_starts(cap, width)[1]


def picks(own_ref, cap, slots, members, count):
    rows = whole(cap)
    source, slot = own_ref[0:1, :members], own_ref[8:9, :members]
    index = iota((slots, members), 0) - source * rows
    found = [(index == slot) & (slot < rows)]
    for part in range(count):
        found.append((index == slot - rows + part * (cap % 8)) & (slot >= rows))
    return [one.astype(BF16) for one in found]


def fill(own_ref, cap, q_ref, k_ref, v_ref, out_ref):
    base = q_ref.shape[1] + 2 * HD
    starts, size = part_starts(cap, base)
    given = jnp.concatenate([q_ref[...], k_ref[...], v_ref[...]], axis=1)
    pick, *parts = picks(own_ref, cap, out_ref.shape[0], q_ref.shape[0], len(starts))
    out_ref[:, :base] = dot(pick, given).astype(BF16)
    if parts:
        total = None
        for start, part in zip(starts, parts):
            piece = given[:, start : start + size]
            if piece.shape[1] < size:
                piece = jnp.concatenate([piece, jnp.zeros((piece.shape[0], size - piece.shape[1]), BF16)], axis=1)
            term = dot(part, piece)
            total = term if total is None else total + term
        out_ref[:, base:] = total.astype(BF16)


def prepare_kernel(cross, caps, *refs):
    given, (sent_ref, own_ref, tables_ref, level_ref), held, sems = refs[:4], refs[4:8], refs[8:12], refs[12]
    copies = [pltpu.make_async_copy(a, b, sems.at[i]) for i, (a, b) in enumerate(zip(given, held))]
    for copy in copies:
        copy.start()
    anc_ref, q_ref, k_ref, v_ref = held
    lines = anc_ref.shape[0]
    members = q_ref.shape[0]
    groups = lines * cross
    z, x = lax.axis_index("z"), lax.axis_index("x")
    copies[0].wait()
    anc = anc_ref[...]
    source = anc // members
    place = iota(anc.shape, 1) % members
    slot = jnp.zeros(anc.shape, jnp.int32)
    for k in range(1, members):
        slot += ((source == pltpu.roll(source, k, 1)) & (place >= k)).astype(jnp.int32)
    need = jnp.max(slot) + 1
    level_ref[0] = sum((need > c).astype(jnp.int32) for c in caps[:-1])
    inside = iota((groups, LANES), 1) < members

    def by_group(a):
        turns = [a] + [pltpu.roll(a, LANES - members * j, 1) for j in range(1, cross)]
        return jnp.where(inside, jnp.concatenate(turns, axis=0), -1)

    source, local, slot = by_group(source), by_group(anc % members), by_group(slot)
    mine = source == z * cross + x
    tables_ref[:, :LANES] = jnp.where(mine, slot, -1).astype(F32).astype(BF16)
    tables_ref[:, LANES:] = local.astype(F32).astype(BF16)
    here = iota((groups, LANES), 0) == x * lines + z
    own_ref[0:8] = jnp.broadcast_to(jnp.sum(jnp.where(here, source, 0), axis=0, keepdims=True), (8, LANES))
    own_ref[8:16] = jnp.broadcast_to(jnp.sum(jnp.where(here, slot, 0), axis=0, keepdims=True), (8, LANES))
    for copy in copies[1:]:
        copy.wait()
    fill(own_ref, FIRST, q_ref, k_ref, v_ref, sent_ref)


def pack_kernel(cap, own_ref, q_ref, k_ref, v_ref, sent_ref):
    fill(own_ref, cap, q_ref, k_ref, v_ref, sent_ref)


def unpack_kernel(cap, own_ref, returned_ref, out_ref):
    members = out_ref.shape[-2]
    width = out_ref.shape[-1]
    starts, _ = part_starts(cap, width)
    pick, *parts = picks(own_ref, cap, returned_ref.shape[0], members, len(starts))
    rows = dot_tn(pick, returned_ref[:, :width])
    if parts:
        rows += jnp.concatenate([dot_tn(part, returned_ref[:, width:]) for part in parts], axis=1)
    rows = rows.astype(BF16)
    for i in range(out_ref.shape[0]):
        out_ref[i] = rows


def attend_kernel(
    cap, cross, tables_ref, recv_ref, keys_ref, values_ref, out_ref,
    keys, values, order, order_smem, total, sems, order_sem,
):
    load_keys = pltpu.make_async_copy(keys_ref, keys, sems.at[0])
    load_values = pltpu.make_async_copy(values_ref, values, sems.at[1])
    load_keys.start()
    load_values.start()
    deep = whole(cap)
    base_rows = recv_ref.shape[0]
    rows = base_rows if cap == deep else 2 * base_rows
    groups = tables_ref.shape[0]
    lines = groups // cross
    extra = cap - deep
    width = total.shape[1] // (8 + extra) * 8
    heads = width // HD
    everything = width + 2 * HD
    scale = math.log2(math.e) / math.sqrt(HD)

    group = iota((rows, groups), 0) % base_rows // deep
    repeat = ((group % cross) * lines + group // cross == iota((rows, groups), 1)).astype(BF16)
    spread = dot(repeat, tables_ref[...])
    index = iota((rows, LANES), 0)
    slot = index % deep
    if cap != deep:
        slot = jnp.where(index < base_rows, slot, jnp.where(slot < extra, slot + deep, -2))
    hit = spread[:, :LANES] == slot.astype(F32)
    local = jnp.sum(jnp.where(hit, spread[:, LANES:] + 1.0, 0.0), axis=1, keepdims=True) - 1.0

    member = (local == iota((rows, LANES), 1).astype(F32)).astype(F32)
    before = (iota((rows, rows), 1) < iota((rows, rows), 0)).astype(BF16)
    rank = dot(before, member.astype(BF16))
    count = jnp.sum(member, axis=0, keepdims=True)
    blocks = jnp.floor((count + (ROWS - 1)) * (1.0 / ROWS))
    upto = (iota((LANES, LANES), 0) < iota((LANES, LANES), 1)).astype(BF16)
    first = dot(jnp.broadcast_to(blocks, (8, LANES)).astype(BF16), upto)[0:1]
    position = jnp.sum(member * (rank + first * ROWS), axis=1, keepdims=True)
    position = jnp.where(local >= 0.0, position, -1.0)
    position_row = jnp.transpose(jnp.broadcast_to(position, (rows, LANES)))[0:1]
    steps = jnp.maximum((jnp.sum(blocks).astype(jnp.int32) + BLOCKS - 1) // BLOCKS, 1)
    ended = (first + blocks) <= iota((LANES, LANES), 0).astype(F32)
    owner = jnp.sum(jnp.where(ended & (iota((LANES, LANES), 1) < groups), 1.0, 0.0), axis=1, keepdims=True)
    owner = jnp.minimum(owner, groups - 1.0)
    order[...] = jnp.transpose(jnp.broadcast_to(owner, (LANES, LANES)))[0:8].astype(jnp.int32)
    move = pltpu.make_async_copy(order, order_smem, order_sem)
    move.start()
    total[...] = jnp.zeros_like(total)

    def step(k, carry):
        base = (k * (BLOCKS * ROWS)).astype(F32)
        taken = (position - base == iota((rows, BLOCKS * ROWS), 1).astype(F32)).astype(BF16)
        across = (position_row - base == iota((BLOCKS * ROWS, rows), 0).astype(F32)).astype(BF16)
        gathered = dot(across[:, :base_rows], recv_ref[:, :everything])
        if cap != deep:
            starts, _ = part_starts(cap, everything)
            behind = across[:, base_rows:].astype(F32)
            pieces = [
                dot(pltpu.roll(behind, part * extra, 1).astype(BF16), recv_ref[:, everything:])
                for part in range(len(starts))
            ]
            gathered += jnp.concatenate(pieces, axis=1)[:, :everything]
        gathered = gathered.astype(BF16)

        @pl.when(k == 0)
        def _():
            move.wait()
            load_keys.wait()
            load_values.wait()

        results = []
        for b in range(BLOCKS):
            ancestor = order_smem[0, k * BLOCKS + b]
            part = gathered[b * ROWS : (b + 1) * ROWS]
            query = jnp.concatenate([part[:, h * HD : (h + 1) * HD] for h in range(heads)], axis=0)
            new_key = jnp.concatenate([part[:, heads * HD : (heads + 1) * HD]] * heads, axis=0)
            new_value = jnp.concatenate([part[:, (heads + 1) * HD :]] * heads, axis=0)
            past = dot_nt(query, keys[ancestor])
            own = jnp.sum(query.astype(F32) * new_key.astype(F32), axis=1, keepdims=True)
            top = jnp.maximum(jnp.max(past, axis=1, keepdims=True), own)
            weight = jnp.exp2((past - top) * scale)
            own = jnp.exp2((own - top) * scale)
            norm = jnp.sum(weight, axis=1, keepdims=True) + own
            mix = dot(weight.astype(BF16), values[ancestor])
            mix = mix + own.astype(BF16).astype(F32) * new_value.astype(F32)
            mix = (mix / norm).astype(BF16)
            results.append(
                jnp.concatenate([mix[h * ROWS : (h + 1) * ROWS] for h in range(heads)], axis=1)
            )
        result = jnp.concatenate(results, axis=0)
        total[:, :width] += dot(taken[:base_rows], result)
        if cap != deep:
            starts, size = part_starts(cap, width)
            behind = taken[base_rows:].astype(F32)
            total[:, width:] += sum(
                dot(pltpu.roll(behind, part * extra, 0).astype(BF16), result[:, start : start + size])
                for part, start in enumerate(starts)
            )
        return carry

    lax.fori_loop(0, steps, step, 0)
    out_ref[...] = total[...].astype(BF16)


def project_kernel(cross, rows_ref, *refs):
    x = lax.axis_index("x")
    for j in range(cross):
        refs[-1][lax.rem(x + j, cross)] = dot(rows_ref[...], refs[j][...]).astype(BF16)


def ring(n, by):
    return [(i, (i + by) % n) for i in range(n)]


def on_device(queries, new_keys, new_values, cache_keys, cache_values, ancestors, out_weight):
    lines = lax.axis_size("z")
    cross = lax.axis_size("x")
    groups = lines * cross
    members = cache_keys.shape[0]
    span = cross * members
    width = queries.shape[1]
    columns = out_weight.shape[1]
    everything = width + 2 * HD

    weights = [out_weight] + [lax.ppermute(out_weight, "x", ring(cross, cross - by)) for by in (1, cross - 1)]

    caps = (FIRST, 9, 10, 12, 16, members)
    inputs = (ancestors.reshape(lines, span), queries, new_keys, new_values)
    sent, own, tables, level = call(
        functools.partial(prepare_kernel, cross, caps),
        "prepare",
        out=[
            jax.ShapeDtypeStruct((groups * FIRST, everything), BF16),
            jax.ShapeDtypeStruct((16, LANES), jnp.int32),
            jax.ShapeDtypeStruct((groups, 2 * LANES), BF16),
            jax.ShapeDtypeStruct((1,), jnp.int32),
        ],
        n_hbm=4,
        out_specs=[pl.BlockSpec(memory_space=VMEM)] * 3 + [pl.BlockSpec(memory_space=pltpu.SMEM)],
        scratch=[pltpu.VMEM(a.shape, a.dtype) for a in inputs] + [pltpu.SemaphoreType.DMA((4,))],
    )(*inputs)

    def exchange(cap):
        rows = whole(cap)
        packed = sent
        if cap != FIRST:
            packed = call(
                functools.partial(pack_kernel, cap),
                "pack",
                out=jax.ShapeDtypeStruct((groups * rows, lanes(cap, everything)), BF16),
                n_vmem=4,
            )(own, queries, new_keys, new_values)
        received = lax.all_to_all(packed.reshape(groups, rows, -1), DOM, 0, 0, tiled=True)
        mixed = call(
            functools.partial(attend_kernel, cap, cross),
            "attend",
            out=jax.ShapeDtypeStruct((groups * rows, lanes(cap, width)), BF16),
            n_vmem=2,
            n_hbm=2,
            scratch=[
                pltpu.VMEM(cache_keys.shape, BF16),
                pltpu.VMEM(cache_values.shape, BF16),
                pltpu.VMEM((8, LANES), jnp.int32),
                pltpu.SMEM((8, LANES), jnp.int32),
                pltpu.VMEM((groups * rows, lanes(cap, width)), F32),
                pltpu.SemaphoreType.DMA((2,)),
                pltpu.SemaphoreType.DMA,
            ],
            limit=40,
        )(tables, received.reshape(groups * rows, -1), cache_keys, cache_values)
        returned = lax.all_to_all(mixed.reshape(groups, rows, -1), DOM, 0, 0, tiled=True)
        return call(
            functools.partial(unpack_kernel, cap),
            "unpack",
            out=jax.ShapeDtypeStruct((lines, members, width), BF16),
            n_vmem=2,
        )(own, returned.reshape(groups * rows, -1))

    heads_out = lax.switch(level[0], [functools.partial(exchange, c) for c in caps])

    heads_out, *weights = lax.optimization_barrier((heads_out, *weights))
    weights.insert(2, lax.ppermute(weights[1], "x", ring(cross, cross - 1)))
    column = lax.all_to_all(heads_out, "z", 0, 0, tiled=True).reshape(lines * members, width)
    partial_rows = call(
        functools.partial(project_kernel, cross),
        "project",
        out=jax.ShapeDtypeStruct((cross, lines * members, columns), BF16),
        n_vmem=1 + cross,
    )(column, *weights)
    shares = lax.all_to_all(
        partial_rows.reshape(cross * lines, members, columns), ("x",) + TP, 0, 0, tiled=True
    )
    summed = jnp.sum(shares.reshape(cross, lines, members, columns).astype(F32), axis=1)
    return summed.reshape(cross * members, columns).astype(BF16)


def solution(mesh):
    inner = Mesh(mesh.devices.reshape(8, 4, 4, 2), DOM + TP)
    return jax.shard_map(
        on_device,
        mesh=inner,
        in_specs=(P(DOM, TP), P(DOM, TP), P(DOM, TP), P(DOM, None, TP), P(DOM, None, TP), P(), P(TP, DOM)),
        out_specs=P(TP, DOM),
        check_vma=False,
    )
```

```python
import functools
import math

import jax
import jax.numpy as jnp
from jax import lax
from jax.experimental import pallas as pl
from jax.experimental.pallas import tpu as pltpu
from jax.sharding import Mesh, PartitionSpec as P

HD = 128
ROWS = 16
BLOCKS = 11
LANES = 128
FIRST = 8
VMEM = pltpu.VMEM
F32 = jnp.float32
BF16 = jnp.bfloat16
DOM = ("z", "x")
TP = ("y", "core")


def iota(shape, dim):
    return lax.broadcasted_iota(jnp.int32, shape, dim)


def dot(a, b):
    return jnp.dot(a, b, preferred_element_type=F32)


def dot_tn(a, b):
    return lax.dot_general(a, b, (((0,), (0,)), ((), ())), preferred_element_type=F32)


def dot_nt(a, b):
    return lax.dot_general(a, b, (((1,), (1,)), ((), ())), preferred_element_type=F32)


def call(body, name, *, out, n_vmem=0, n_hbm=0, scratch=(), limit=24, out_specs=None):
    spaces = [VMEM] * n_vmem + [pltpu.HBM] * n_hbm
    return pl.pallas_call(
        body,
        out_shape=out,
        in_specs=[pl.BlockSpec(memory_space=space) for space in spaces],
        out_specs=out_specs or pl.BlockSpec(memory_space=VMEM),
        scratch_shapes=scratch,
        compiler_params=pltpu.CompilerParams(vmem_limit_bytes=limit << 20),
        name=name,
    )


def whole(cap):
    return cap // 8 * 8


def part_starts(cap, width):
    extra = cap % 8
    if not extra:
        return (), 0
    size = -(-(width // HD) * extra // 8) * HD
    return tuple(range(0, width, size)), size


def lanes(cap, width):
    return width + part_starts(cap, width)[1]


def picks(own_ref, cap, slots, members, count):
    rows = whole(cap)
    source, slot = own_ref[0:1, :members], own_ref[8:9, :members]
    index = iota((slots, members), 0) - source * rows
    found = [(index == slot) & (slot < rows)]
    for part in range(count):
        found.append((index == slot - rows + part * (cap % 8)) & (slot >= rows))
    return [one.astype(BF16) for one in found]


def fill(own_ref, cap, q_ref, k_ref, v_ref, out_ref):
    base = q_ref.shape[1] + 2 * HD
    starts, size = part_starts(cap, base)
    given = jnp.concatenate([q_ref[...], k_ref[...], v_ref[...]], axis=1)
    pick, *parts = picks(own_ref, cap, out_ref.shape[0], q_ref.shape[0], len(starts))
    out_ref[:, :base] = dot(pick, given).astype(BF16)
    if parts:
        total = None
        for start, part in zip(starts, parts):
            piece = given[:, start : start + size]
            if piece.shape[1] < size:
                piece = jnp.concatenate([piece, jnp.zeros((piece.shape[0], size - piece.shape[1]), BF16)], axis=1)
            term = dot(part, piece)
            total = term if total is None else total + term
        out_ref[:, base:] = total.astype(BF16)


def prepare_kernel(cross, caps, *refs):
    given, (sent_ref, own_ref, tables_ref, level_ref), held, sems = refs[:4], refs[4:8], refs[8:12], refs[12]
    copies = [pltpu.make_async_copy(a, b, sems.at[i]) for i, (a, b) in enumerate(zip(given, held))]
    for copy in copies:
        copy.start()
    anc_ref, q_ref, k_ref, v_ref = held
    lines = anc_ref.shape[0]
    members = q_ref.shape[0]
    groups = lines * cross
    z, x = lax.axis_index("z"), lax.axis_index("x")
    copies[0].wait()
    anc = anc_ref[...]
    source = anc // members
    place = iota(anc.shape, 1) % members
    slot = jnp.zeros(anc.shape, jnp.int32)
    for k in range(1, members):
        slot += ((source == pltpu.roll(source, k, 1)) & (place >= k)).astype(jnp.int32)
    need = jnp.max(slot) + 1
    level_ref[0] = sum((need > c).astype(jnp.int32) for c in caps[:-1])
    inside = iota((groups, LANES), 1) < members

    def by_group(a):
        turns = [a] + [pltpu.roll(a, LANES - members * j, 1) for j in range(1, cross)]
        return jnp.where(inside, jnp.concatenate(turns, axis=0), -1)

    source, local, slot = by_group(source), by_group(anc % members), by_group(slot)
    mine = source == z * cross + x
    tables_ref[:, :LANES] = jnp.where(mine, slot, -1).astype(F32).astype(BF16)
    tables_ref[:, LANES:] = local.astype(F32).astype(BF16)
    here = iota((groups, LANES), 0) == x * lines + z
    own_ref[0:8] = jnp.broadcast_to(jnp.sum(jnp.where(here, source, 0), axis=0, keepdims=True), (8, LANES))
    own_ref[8:16] = jnp.broadcast_to(jnp.sum(jnp.where(here, slot, 0), axis=0, keepdims=True), (8, LANES))
    for copy in copies[1:]:
        copy.wait()
    fill(own_ref, FIRST, q_ref, k_ref, v_ref, sent_ref)


def pack_kernel(cap, own_ref, q_ref, k_ref, v_ref, sent_ref):
    fill(own_ref, cap, q_ref, k_ref, v_ref, sent_ref)


def unpack_kernel(cap, own_ref, returned_ref, out_ref):
    members = out_ref.shape[-2]
    width = out_ref.shape[-1]
    starts, _ = part_starts(cap, width)
    pick, *parts = picks(own_ref, cap, returned_ref.shape[0], members, len(starts))
    rows = dot_tn(pick, returned_ref[:, :width])
    if parts:
        rows += jnp.concatenate([dot_tn(part, returned_ref[:, width:]) for part in parts], axis=1)
    rows = rows.astype(BF16)
    for i in range(out_ref.shape[0]):
        out_ref[i] = rows


def attend_kernel(
    cap, cross, tables_ref, recv_ref, keys_ref, values_ref, out_ref,
    keys, values, order, order_smem, total, sems, order_sem,
):
    load_keys = pltpu.make_async_copy(keys_ref, keys, sems.at[0])
    load_values = pltpu.make_async_copy(values_ref, values, sems.at[1])
    load_keys.start()
    load_values.start()
    deep = whole(cap)
    base_rows = recv_ref.shape[0]
    rows = base_rows if cap == deep else 2 * base_rows
    groups = tables_ref.shape[0]
    lines = groups // cross
    extra = cap - deep
    width = total.shape[1] // (8 + extra) * 8
    heads = width // HD
    everything = width + 2 * HD
    scale = math.log2(math.e) / math.sqrt(HD)

    group = iota((rows, groups), 0) % base_rows // deep
    repeat = ((group % cross) * lines + group // cross == iota((rows, groups), 1)).astype(BF16)
    spread = dot(repeat, tables_ref[...])
    index = iota((rows, LANES), 0)
    slot = index % deep
    if cap != deep:
        slot = jnp.where(index < base_rows, slot, jnp.where(slot < extra, slot + deep, -2))
    hit = spread[:, :LANES] == slot.astype(F32)
    local = jnp.sum(jnp.where(hit, spread[:, LANES:] + 1.0, 0.0), axis=1, keepdims=True) - 1.0

    member = (local == iota((rows, LANES), 1).astype(F32)).astype(F32)
    before = (iota((rows, rows), 1) < iota((rows, rows), 0)).astype(BF16)
    rank = dot(before, member.astype(BF16))
    count = jnp.sum(member, axis=0, keepdims=True)
    blocks = jnp.floor((count + (ROWS - 1)) * (1.0 / ROWS))
    upto = (iota((LANES, LANES), 0) < iota((LANES, LANES), 1)).astype(BF16)
    first = dot(jnp.broadcast_to(blocks, (8, LANES)).astype(BF16), upto)[0:1]
    position = jnp.sum(member * (rank + first * ROWS), axis=1, keepdims=True)
    position = jnp.where(local >= 0.0, position, -1.0)
    position_row = jnp.transpose(jnp.broadcast_to(position, (rows, LANES)))[0:1]
    steps = jnp.maximum((jnp.sum(blocks).astype(jnp.int32) + BLOCKS - 1) // BLOCKS, 1)
    ended = (first + blocks) <= iota((LANES, LANES), 0).astype(F32)
    owner = jnp.sum(jnp.where(ended & (iota((LANES, LANES), 1) < groups), 1.0, 0.0), axis=1, keepdims=True)
    owner = jnp.minimum(owner, groups - 1.0)
    order[...] = jnp.transpose(jnp.broadcast_to(owner, (LANES, LANES)))[0:8].astype(jnp.int32)
    move = pltpu.make_async_copy(order, order_smem, order_sem)
    move.start()
    total[...] = jnp.zeros_like(total)

    def step(k, carry):
        base = (k * (BLOCKS * ROWS)).astype(F32)
        taken = (position - base == iota((rows, BLOCKS * ROWS), 1).astype(F32)).astype(BF16)
        across = (position_row - base == iota((BLOCKS * ROWS, rows), 0).astype(F32)).astype(BF16)
        gathered = dot(across[:, :base_rows], recv_ref[:, :everything])
        if cap != deep:
            starts, _ = part_starts(cap, everything)
            behind = across[:, base_rows:].astype(F32)
            pieces = [
                dot(pltpu.roll(behind, part * extra, 1).astype(BF16), recv_ref[:, everything:])
                for part in range(len(starts))
            ]
            gathered += jnp.concatenate(pieces, axis=1)[:, :everything]
        gathered = gathered.astype(BF16)

        @pl.when(k == 0)
        def _():
            move.wait()
            load_keys.wait()
            load_values.wait()

        results = []
        for b in range(BLOCKS):
            ancestor = order_smem[0, k * BLOCKS + b]
            part = gathered[b * ROWS : (b + 1) * ROWS]
            query = jnp.concatenate([part[:, h * HD : (h + 1) * HD] for h in range(heads)], axis=0)
            new_key = jnp.concatenate([part[:, heads * HD : (heads + 1) * HD]] * heads, axis=0)
            new_value = jnp.concatenate([part[:, (heads + 1) * HD :]] * heads, axis=0)
            past = dot_nt(query, keys[ancestor])
            own = jnp.sum(query.astype(F32) * new_key.astype(F32), axis=1, keepdims=True)
            top = jnp.maximum(jnp.max(past, axis=1, keepdims=True), own)
            weight = jnp.exp2((past - top) * scale)
            own = jnp.exp2((own - top) * scale)
            norm = jnp.sum(weight, axis=1, keepdims=True) + own
            mix = dot(weight.astype(BF16), values[ancestor])
            mix = mix + own.astype(BF16).astype(F32) * new_value.astype(F32)
            mix = (mix / norm).astype(BF16)
            results.append(
                jnp.concatenate([mix[h * ROWS : (h + 1) * ROWS] for h in range(heads)], axis=1)
            )
        result = jnp.concatenate(results, axis=0)
        total[:, :width] += dot(taken[:base_rows], result)
        if cap != deep:
            starts, size = part_starts(cap, width)
            behind = taken[base_rows:].astype(F32)
            total[:, width:] += sum(
                dot(pltpu.roll(behind, part * extra, 0).astype(BF16), result[:, start : start + size])
                for part, start in enumerate(starts)
            )
        return carry

    lax.fori_loop(0, steps, step, 0)
    out_ref[...] = total[...].astype(BF16)


def project_kernel(cross, rows_ref, *refs):
    x = lax.axis_index("x")
    out_ref = refs[-1]
    lines, _, members, _ = out_ref.shape
    for j in range(cross):
        share = dot(rows_ref[...], refs[j][...]).astype(BF16)
        for line in range(lines):
            out_ref[line, lax.rem(x + j, cross)] = share[line * members : (line + 1) * members]


def ring(n, by):
    return [(i, (i + by) % n) for i in range(n)]


def on_device(queries, new_keys, new_values, cache_keys, cache_values, ancestors, out_weight):
    lines = lax.axis_size("z")
    cross = lax.axis_size("x")
    groups = lines * cross
    members = cache_keys.shape[0]
    span = cross * members
    width = queries.shape[1]
    columns = out_weight.shape[1]
    everything = width + 2 * HD

    weights = [out_weight] + [lax.ppermute(out_weight, "x", ring(cross, cross - by)) for by in (1, cross - 1)]

    caps = (FIRST, 9, 10, 12, 16, members)
    inputs = (ancestors.reshape(lines, span), queries, new_keys, new_values)
    sent, own, tables, level = call(
        functools.partial(prepare_kernel, cross, caps),
        "prepare",
        out=[
            jax.ShapeDtypeStruct((groups * FIRST, everything), BF16),
            jax.ShapeDtypeStruct((16, LANES), jnp.int32),
            jax.ShapeDtypeStruct((groups, 2 * LANES), BF16),
            jax.ShapeDtypeStruct((1,), jnp.int32),
        ],
        n_hbm=4,
        out_specs=[pl.BlockSpec(memory_space=VMEM)] * 3 + [pl.BlockSpec(memory_space=pltpu.SMEM)],
        scratch=[pltpu.VMEM(a.shape, a.dtype) for a in inputs] + [pltpu.SemaphoreType.DMA((4,))],
    )(*inputs)

    def exchange(cap):
        rows = whole(cap)
        packed = sent
        if cap != FIRST:
            packed = call(
                functools.partial(pack_kernel, cap),
                "pack",
                out=jax.ShapeDtypeStruct((groups * rows, lanes(cap, everything)), BF16),
                n_vmem=4,
            )(own, queries, new_keys, new_values)
        received = lax.all_to_all(packed.reshape(groups, rows, -1), DOM, 0, 0, tiled=True)
        mixed = call(
            functools.partial(attend_kernel, cap, cross),
            "attend",
            out=jax.ShapeDtypeStruct((groups * rows, lanes(cap, width)), BF16),
            n_vmem=2,
            n_hbm=2,
            scratch=[
                pltpu.VMEM(cache_keys.shape, BF16),
                pltpu.VMEM(cache_values.shape, BF16),
                pltpu.VMEM((8, LANES), jnp.int32),
                pltpu.SMEM((8, LANES), jnp.int32),
                pltpu.VMEM((groups * rows, lanes(cap, width)), F32),
                pltpu.SemaphoreType.DMA((2,)),
                pltpu.SemaphoreType.DMA,
            ],
            limit=40,
        )(tables, received.reshape(groups * rows, -1), cache_keys, cache_values)
        returned = lax.all_to_all(mixed.reshape(groups, rows, -1), DOM, 0, 0, tiled=True)
        return call(
            functools.partial(unpack_kernel, cap),
            "unpack",
            out=jax.ShapeDtypeStruct((lines, members, width), BF16),
            n_vmem=2,
        )(own, returned.reshape(groups * rows, -1))

    heads_out = lax.switch(level[0], [functools.partial(exchange, c) for c in caps])

    heads_out, *weights = lax.optimization_barrier((heads_out, *weights))
    weights.insert(2, lax.ppermute(weights[1], "x", ring(cross, cross - 1)))
    column = lax.all_to_all(heads_out, "z", 0, 0, tiled=True).reshape(lines * members, width)
    partial_rows = call(
        functools.partial(project_kernel, cross),
        "project",
        out=jax.ShapeDtypeStruct((lines, cross, members, columns), BF16),
        n_vmem=1 + cross,
    )(column, *weights)
    shares = lax.all_to_all(
        partial_rows.reshape(cross * lines, members, columns), TP + ("x",), 0, 0, tiled=True
    )
    summed = jnp.sum(shares.reshape(lines, cross, members, columns).astype(F32), axis=0)
    return summed.reshape(cross * members, columns).astype(BF16)


def solution(mesh):
    inner = Mesh(mesh.devices.reshape(8, 4, 4, 2), DOM + TP)
    return jax.shard_map(
        on_device,
        mesh=inner,
        in_specs=(P(DOM, TP), P(DOM, TP), P(DOM, TP), P(DOM, None, TP), P(DOM, None, TP), P(), P(TP, DOM)),
        out_specs=P(TP, DOM),
        check_vma=False,
    )
```
